512 devices in a mesh: gx: 16 (over z_lo, y), gy: 32 (over z_hi, x, core).
Axes of the slice: x: 4, y: 8, z: 8 (z_hi: 4, z_lo: 2; z = z_hi * 2 + z_lo), core: 2. Of those that a mesh axis runs over, the one named last changes fastest.
Arguments:
- positions: float32 [16, 32, 3, 384], P('gx', 'gy'), may hold values from 0 to 36, as said below
- features: bfloat16 [16, 32, 128, 384], P('gx', 'gy'), may hold values from -12 to 12
- nbr_tiles: int32 [16, 32, 3, 32], P('gx', 'gy'), may hold values from 0 to 27, as said below
- kvec_index: int32 [3, 4096], replicated, may hold values from -8 to 8, as said below
- weight_charge: bfloat16 [16, 128], replicated, may hold values from -0.5 to 0.5
- weight_pair: bfloat16 [16, 128], replicated, may hold values from -0.5 to 0.5
Outputs:
- energy: float32 [], replicated
- forces: float32 [16, 32, 3, 384], P('gx', 'gy')
The draws below stay inside these ranges and needn't reach their ends.
Inputs may be any that keep to these rules, and one draw needn't show every extreme that they name: `nbr_tiles`: an entry below 27 names a tile of the neighbourhood, each at most once in a row; 27 marks an empty slot. `kvec_index`: the third component is 1 or more. `positions`: atoms of block b of a column have z between 12 b and 12 (b + 1); x and y lie between 0 and 10.
All inputs are finite; a program needn't handle non-finite values.
Results may differ from the reference program's by a relative error of at most 0.0055.
Values sent between devices are 32-bit elements; how exact they have to be, the bound alone decides.
A program may use at most 64 MiB of HBM per device.

```python
import math
import jax
import jax.numpy as jnp
from jax import lax

ATOMS = 384
TILE = 128
SLOTS = 32
FEAT = 128
QCH = 16
PCH = 16
KVEC = 4096
NMAX = 8
NBLK = 3
COLS_X = 16
COLS_Y = 32


def draw_positions(key, part):
    key = jax.random.fold_in(key, 11)
    first, second, third = jax.random.split(key, 3)
    shape = (COLS_X, COLS_Y, ATOMS)
    unit_x = jax.random.uniform(first, shape, jnp.float32)
    unit_y = jax.random.uniform(second, shape, jnp.float32)
    unit_z = jax.random.uniform(third, shape, jnp.float32)
    blocks = (jnp.arange(ATOMS) // TILE).astype(jnp.float32)
    depth = (blocks[None, None, :] + unit_z) * 12.0
    return jnp.stack([unit_x * 10.0, unit_y * 10.0, depth], axis=2).astype(jnp.float32)


def feature_field(key, low, high):
    noise_key, mean_key = jax.random.split(key)
    noise = jnp.clip(jax.random.normal(noise_key, (COLS_X, COLS_Y, FEAT, ATOMS), jnp.float32), -4.0, 4.0)
    common = jnp.clip(0.7 * jax.random.normal(mean_key, (FEAT,), jnp.float32), -3.0, 3.0)
    column = jnp.arange(COLS_X * COLS_Y).astype(jnp.float32) / (COLS_X * COLS_Y - 1)
    scale = (low + (high - low) * column).reshape(COLS_X, COLS_Y, 1, 1)
    values = scale * (noise + common[None, None, :, None])
    return jnp.clip(values, -12.0, 12.0)


def draw_features(key, part):
    key = jax.random.fold_in(key, 53)
    values = feature_field(key, 0.6, 1.2)
    return values.astype(jnp.bfloat16)


def draw_nbr_tiles(key, part):
    key = jax.random.fold_in(key, 23)
    shuffle_key, drop_key, count_key = jax.random.split(key, 3)
    block = jnp.arange(NBLK)
    hoods = jnp.arange(9)
    steps = jnp.array([-1, 0, 1])
    near = hoods[None, :, None] * NBLK + (block[:, None, None] + steps[None, None, :]) % NBLK
    near = jnp.broadcast_to(near.reshape(1, 1, NBLK, 27), (COLS_X, COLS_Y, NBLK, 27)).astype(jnp.int32)
    rest = near[..., 1:]
    drop_scores = jax.random.randint(drop_key, (COLS_X, COLS_Y, NBLK, 26), 0, 1 << 20) * 32 + jnp.arange(26)
    drop_order = jnp.argsort(drop_scores, axis=-1, stable=True)
    drop_rank = jnp.argsort(drop_order, axis=-1, stable=True)
    counts = jax.random.randint(count_key, (COLS_X, COLS_Y, NBLK, 1), 3, 9)
    rest = jnp.where(drop_rank < counts, 9 * NBLK, rest)
    empty = jnp.full((COLS_X, COLS_Y, NBLK, SLOTS - 27), 9 * NBLK, jnp.int32)
    entries = jnp.concatenate([near[..., :1], rest, empty], axis=-1).astype(jnp.int32)
    scores = jax.random.randint(shuffle_key, (COLS_X, COLS_Y, NBLK, SLOTS), 0, 1 << 20) * SLOTS + jnp.arange(SLOTS)
    order = jnp.argsort(scores, axis=-1, stable=True)
    return jnp.take_along_axis(entries, order, axis=-1).astype(jnp.int32)


def draw_kvec_index(key, part):
    key = jax.random.fold_in(key, 37)
    first, second = jax.random.split(key)
    plane = jax.random.randint(first, (2, KVEC), -NMAX, NMAX + 1)
    upper = jax.random.randint(second, (1, KVEC), 1, NMAX + 1)
    index = jnp.concatenate([plane, upper], axis=0)
    index = index.at[0, 0].set(NMAX).at[0, 1].set(-NMAX)
    return index.astype(jnp.int32)


def scatter_about(stream_key, extent, scale, most, held_as=jnp.bfloat16):
    return jnp.clip(scale * jax.random.normal(stream_key, extent, jnp.float32), -most, most).astype(held_as)


def setup_inputs(seed: int = 0) -> dict:
    splits = jax.random.split(jax.random.key(seed), 7)
    positions = draw_positions(jax.random.fold_in(splits[6], 71), 0)
    features = draw_features(jax.random.fold_in(splits[6], 71), 0)
    nbr_tiles = draw_nbr_tiles(jax.random.fold_in(splits[6], 71), 0)
    kvec_index = draw_kvec_index(jax.random.fold_in(splits[6], 71), 0)
    weight_charge = scatter_about(splits[4], (QCH, FEAT), FEAT ** -0.5, 0.5)
    weight_pair = scatter_about(splits[5], (PCH, FEAT), FEAT ** -0.5, 0.5)
    return {"positions": positions, "features": features, "nbr_tiles": nbr_tiles, "kvec_index": kvec_index, "weight_charge": weight_charge, "weight_pair": weight_pair}


column_width = 10.0
slab_depth = 12.0
cutoff = 5.0
smear = 1.5
pair_scale = 0.25

def block_terms(own_pos, own_feat, tile_pos, tile_feat, row, block, nblk, depth):
    tile = own_pos.shape[1]
    picked_pos = jnp.take(tile_pos, row, axis=0)
    picked_feat = jnp.take(tile_feat, row, axis=0)
    coupling = jnp.einsum('ci,ncj->nij', own_feat, picked_feat, precision=lax.Precision.HIGHEST)
    delta = own_pos[None, :, :, None] - picked_pos[:, :, None, :]
    along_z = delta[:, 2]
    along_z = along_z - depth * jnp.floor(along_z / depth + 0.5)
    dist = (delta[:, 0] * delta[:, 0] + delta[:, 1] * delta[:, 1] + along_z * along_z) / (cutoff * cutoff)
    weight = jnp.maximum(1.0 - dist, 0.0)
    valid = (row < 9 * nblk).astype(jnp.float32)
    same = (row == 4 * nblk + block).astype(jnp.float32)
    ident = jnp.eye(tile, dtype=jnp.float32)
    mask = valid[:, None, None] * (1.0 - same[:, None, None] * ident[None])
    coupling = coupling * mask
    energy = 0.5 * pair_scale * jnp.sum(coupling * weight * weight)
    scaled = coupling * weight
    force_x = lax.optimization_barrier(jnp.sum(scaled * delta[:, 0], axis=(0, 2)))
    force_y = lax.optimization_barrier(jnp.sum(scaled * delta[:, 1], axis=(0, 2)))
    force_z = lax.optimization_barrier(jnp.sum(scaled * along_z, axis=(0, 2)))
    force = 4.0 * pair_scale / (cutoff * cutoff) * jnp.stack([force_x, force_y, force_z])
    return (energy, force)

def make_tiles(hood, nblk, tile, with_shift):
    if with_shift:
        offset = (jnp.arange(3).astype(jnp.float32) - 1.0) * column_width
        xs = hood[:, :, 0] + offset[:, None, None]
        ys = hood[:, :, 1] + offset[None, :, None]
        hood = jnp.stack([xs, ys, hood[:, :, 2]], axis=2)
    chans = hood.shape[2]
    tiles = hood.reshape(9, chans, nblk, tile).transpose(0, 2, 1, 3).reshape(9 * nblk, chans, tile)
    return jnp.concatenate([tiles, jnp.zeros((1, chans, tile), jnp.float32)], axis=0)

def pair_terms(pos_col, feat_col, hood_pos, hood_feat, rows):
    tile = 128
    atoms = pos_col.shape[1]
    nblk = atoms // tile
    depth = nblk * slab_depth
    tile_pos = make_tiles(hood_pos, nblk, tile, True)
    tile_feat = make_tiles(hood_feat, nblk, tile, False)
    own_pos = pos_col.reshape(3, nblk, tile).transpose(1, 0, 2)
    own_feat = feat_col.reshape(feat_col.shape[0], nblk, tile).transpose(1, 0, 2)

    def one_block(items):
        block, opos, ofeat, row = items
        return block_terms(opos, ofeat, tile_pos, tile_feat, row, block, nblk, depth)
    energies, forces = lax.map(one_block, (jnp.arange(nblk).astype(jnp.int32), own_pos, own_feat, rows))
    return (jnp.sum(energies), forces.transpose(1, 0, 2).reshape(3, atoms))

def wave_vectors(kvec_index, box):
    kvec = 2.0 * math.pi * kvec_index.astype(jnp.float32) / box[:, None]
    ksq = lax.optimization_barrier(jnp.sum(kvec * kvec, axis=0))
    return (kvec, 2.0 * jnp.exp(-0.5 * smear * smear * ksq) / ksq)

def trig(glob, kvec):
    theta = lax.dot_general(glob, kvec, (((0,), (0,)), ((), ())), precision=lax.Precision.HIGHEST, preferred_element_type=jnp.float32)
    return (jnp.cos(theta).astype(jnp.bfloat16), jnp.sin(theta).astype(jnp.bfloat16))

def reference(positions, features, nbr_tiles, kvec_index, weight_charge, weight_pair):
    cols_x, cols_y, _, atoms = positions.shape
    nblk = atoms // 128
    ntot = cols_x * cols_y * atoms
    kcount = kvec_index.shape[1]
    norm = 1.0 / math.sqrt(ntot * kcount)
    charges = jnp.einsum('qf,xyfa->xyqa', weight_charge.astype(jnp.float32), features.astype(jnp.float32)).astype(jnp.bfloat16)
    pair_feat = jnp.einsum('pf,xyfa->xypa', weight_pair.astype(jnp.float32), features.astype(jnp.float32))
    shift_x = jnp.arange(cols_x).astype(jnp.float32) * column_width
    shift_y = jnp.arange(cols_y).astype(jnp.float32) * column_width
    glob = jnp.stack([positions[:, :, 0] + shift_x[:, None, None], positions[:, :, 1] + shift_y[None, :, None], positions[:, :, 2]], axis=2)
    box = jnp.array([cols_x * column_width, cols_y * column_width, nblk * slab_depth], jnp.float32)
    kvec, green = wave_vectors(kvec_index, box)
    green = green * norm
    ncol = cols_x * cols_y
    glob_flat = glob.reshape(ncol, 3, atoms)
    charge_flat = charges.reshape(ncol, charges.shape[2], atoms)

    def add_column(total, items):
        gcol, qcol = items
        cs, sn = trig(gcol, kvec)
        part_re = jnp.dot(qcol, cs, preferred_element_type=jnp.float32)
        part_im = jnp.dot(qcol, sn, preferred_element_type=jnp.float32)
        return (total + jnp.stack([part_re, part_im]), None)
    start = jnp.zeros((2, charges.shape[2], kcount), jnp.float32)
    factors, _ = lax.scan(add_column, start, (glob_flat, charge_flat))
    re, im = (factors[0], factors[1])
    e_long = jnp.sum(green[None, :] * (re * re + im * im))
    pf = (2.0 * green[None, :] * re).astype(jnp.bfloat16)
    qf = (2.0 * green[None, :] * im).astype(jnp.bfloat16)

    def long_force(items):
        gcol, qcol = items
        cs, sn = trig(gcol, kvec)
        dims = (((0,), (0,)), ((), ()))
        vc = lax.dot_general(qcol, qf, dims, preferred_element_type=jnp.float32)
        vs = lax.dot_general(qcol, pf, dims, preferred_element_type=jnp.float32)
        wmat = cs.astype(jnp.float32) * vc - sn.astype(jnp.float32) * vs
        grad = lax.dot_general(kvec, wmat, (((1,), (1,)), ((), ())), precision=lax.Precision.HIGHEST, preferred_element_type=jnp.float32)
        return -grad
    force_long = lax.map(long_force, (glob_flat, charge_flat)).reshape(cols_x, cols_y, 3, atoms)

    def hood_of(arr):
        rows = []
        for ix in range(3):
            rows.append(jnp.stack([jnp.roll(arr, (1 - ix, 1 - iy), (0, 1)) for iy in range(3)], axis=2))
        return jnp.stack(rows, axis=2)
    hood_pos = hood_of(positions).reshape((ncol, 3, 3) + positions.shape[2:])
    hood_feat = hood_of(pair_feat).reshape((ncol, 3, 3) + pair_feat.shape[2:])

    def pair_column(items):
        pcol, fcol, hpos, hfeat, rows = items
        return pair_terms(pcol, fcol, hpos, hfeat, rows)
    e_cols, force_pair = lax.map(pair_column, (positions.reshape(ncol, 3, atoms), pair_feat.reshape(ncol, pair_feat.shape[2], atoms), hood_pos, hood_feat, nbr_tiles.reshape((ncol,) + nbr_tiles.shape[2:])))
    e_pair = jnp.sum(e_cols)
    energy = (e_long + e_pair) / ntot
    forces = force_long + force_pair.reshape(cols_x, cols_y, 3, atoms)
    return (energy, forces)
```

```python
import functools
import math

import jax
import jax.numpy as jnp
from jax import lax
from jax.experimental import pallas as pl
from jax.experimental.pallas import tpu as pltpu
from jax.sharding import PartitionSpec as P

WIDTH = 10.0
DEPTH = 12.0
CUT = 5.0
SMEAR = 1.5
SCALE = 0.25
NMAX = 8
TILE = 128
NBLK = 3
ATOMS = NBLK * TILE
QCH = 16
PCH = 16
KVEC = 4096
XS = 4
CORES = 2
TILES_C = 19
TILES_S = 18
ROWS = 8 * (TILES_C + TILES_S)
PAIRS = 8 * TILES_C
PADDED = 320
PART = PADDED // XS
MESH = pl.DeviceIdType.MESH
F32 = jnp.float32
BF16 = jnp.bfloat16
FAR = -1.0e30


def split(value):
    high = value.astype(BF16)
    return high, (value - high.astype(F32)).astype(BF16)


def unit_circle(turns):
    turns = turns - jnp.round(turns)
    half = turns * math.pi
    sq = half * half
    sine = 1.0 / 6227020800.0
    for term in (-1.0 / 39916800.0, 1.0 / 362880.0, -1.0 / 5040.0, 1.0 / 120.0, -1.0 / 6.0, 1.0):
        sine = sine * sq + term
    sine = sine * half
    cosine = 1.0 / 479001600.0
    for term in (-1.0 / 3628800.0, 1.0 / 40320.0, -1.0 / 720.0, 1.0 / 24.0, -0.5, 1.0):
        cosine = cosine * sq + term
    return 1.0 - 2.0 * sine * sine, 2.0 * sine * cosine


def dot3(a, b, dims):
    out = None
    for left, right in ((a[0], b[0]), (a[0], b[1]), (a[1], b[0])):
        term = lax.dot_general(left, right, (dims, ((), ())), preferred_element_type=F32)
        out = term if out is None else out + term
    return out


def kernel(
    sizes,
    pos_ref,
    feat_ref,
    nbr_ref,
    kidx_ref,
    wc_ref,
    wp_ref,
    energy_ref,
    force_ref,
    hood,
    mine,
    recv_c,
    acc_x,
    recv_x,
    sum_x,
    send_y,
    recv_y,
    recv_z,
    gath_y,
    full,
    vf,
    vh,
    vl,
    uf,
    uh,
    ul,
    zrow,
    lf,
    lh,
    ll,
    coef,
    codes,
    fi,
    zi,
    cmask,
    mbuf,
    pbuf,
    acc_p,
    fpair,
    halo_s,
    halo_r,
    rc_s,
    rc_r,
    rx_s,
    rx_r,
    ry_s,
    ry_r,
    rz_s,
    rz_r,
    gy_s,
    gy_r,
    gx_s,
    gx_r,
    gc_s,
    gc_r,
):
    cols_x, cols_y, ys, z_lo_n, z_hi_n = sizes
    zs = z_lo_n * z_hi_n
    sub = PART // ys
    gx = lax.axis_index("gx")
    gy = lax.axis_index("gy")
    z_lo, y = lax.div(gx, ys), lax.rem(gx, ys)
    z_hi = lax.div(gy, XS * CORES)
    x = lax.div(lax.rem(gy, XS * CORES), CORES)
    core = lax.rem(gy, CORES)
    z = z_hi * z_lo_n + z_lo
    other = 1 - core

    def core_dev():
        return (gx, gy + 1 - 2 * core)

    def x_dev(j):
        return (gx, (z_hi * XS + j) * CORES + core)

    def y_dev(j):
        return (z_lo * ys + j, gy)

    def z_dev(j):
        lo, hi = lax.rem(j, z_lo_n), lax.div(j, z_lo_n)
        return (lo * ys + y, (hi * XS + x) * CORES + core)

    def halo_dev(ix, iy):
        return (
            lax.rem(gx + (1 - ix) + cols_x, cols_x),
            lax.rem(gy + (1 - iy) + cols_y, cols_y),
        )

    halo = [(ix, iy) for ix in range(3) for iy in range(3) if (ix, iy) != (1, 1)]
    x_peers = [lax.rem(x + d, XS) for d in range(1, XS)]
    y_peers = [lax.rem(y + d, ys) for d in range(1, ys)]
    z_peers = [lax.rem(z + d, zs) for d in range(1, zs)]

    def copy(src, dst, send, recv, dev):
        return pltpu.make_async_remote_copy(
            src_ref=src, dst_ref=dst, send_sem=send, recv_sem=recv, device_id=dev, device_id_type=MESH
        )

    barrier = pltpu.get_barrier_semaphore()
    partners = [core_dev()]
    partners += [x_dev(j) for j in x_peers]
    partners += [y_dev(j) for j in y_peers]
    partners += [z_dev(j) for j in z_peers]
    partners += [halo_dev(ix, iy) for ix, iy in halo]
    for dev in partners:
        pl.semaphore_signal(barrier, inc=1, device_id=dev, device_id_type=MESH)

    feat = feat_ref[...]
    charges = jnp.dot(wc_ref[...], feat, preferred_element_type=F32).astype(BF16).astype(F32)
    pair_feat = jnp.dot(wp_ref[...], feat, preferred_element_type=F32)
    pos = pos_ref[...]
    hood[4, 0:PCH, :] = pair_feat
    hood[4, PCH:, :] = jnp.zeros((8, ATOMS), F32)
    hood[4, PCH : PCH + 3, :] = pos * (1.0 / CUT)

    order = lax.broadcasted_iota(jnp.int32, (8, ATOMS), 0).astype(F32) + 1.0
    gxf, gyf = gx.astype(F32), gy.astype(F32)
    cx, sx = unit_circle(order * ((pos[0:1] + gxf * WIDTH) * (1.0 / (cols_x * WIDTH))))
    cy, sy = unit_circle(order * ((pos[1:2] + gyf * WIDTH) * (1.0 / (cols_y * WIDTH))))
    cz, sz = unit_circle(order * (pos[2:3] * (1.0 / (NBLK * DEPTH))))

    def row(tile):
        return pl.ds(8 * tile, 8)

    for n in range(1, NMAX + 1):
        cyn, syn = cy[n - 1 : n], sy[n - 1 : n]
        cc, ss, sc, cs = cx * cyn, sx * syn, sx * cyn, cx * syn
        vf[row(8 + n), :] = cc - ss
        vf[row(8 - n), :] = cc + ss
        vf[row(TILES_C + 8 + n), :] = sc + cs
        vf[row(TILES_C + 8 - n), :] = sc - cs
    vf[row(8), :] = cx
    vf[row(TILES_C + 8), :] = sx
    vf[row(17), :] = cy
    vf[row(TILES_C + 17), :] = sy
    vf[row(18), :] = jnp.where(order < 1.5, 1.0, 0.0)
    vf[ROWS:, :] = jnp.zeros((PADDED - ROWS, ATOMS), F32)
    for c in range(QCH):
        uf[row(c), :] = cz * charges[c : c + 1]
        uf[row(QCH + c), :] = sz * charges[c : c + 1]
    high, low = split(vf[...])
    vh[...] = high
    vl[...] = low
    high, low = split(uf[...])
    uh[...] = high
    ul[...] = low

    pl.semaphore_wait(barrier, len(partners))

    core_copies = []
    for d in range(1, XS + 1):
        j = lax.rem(x + d, XS)
        rows = pl.ds(pl.multiple_of(j * PART, PART), PART)
        part = dot3(
            (vh[rows, :], vl[rows, :]), (uh[...], ul[...]), ((1,), (1,))
        )
        mine[0, j] = part[:, :TILE]
        mine[1, j] = part[:, TILE:]
        cp = copy(mine.at[other, j], recv_c.at[j], rc_s.at[j], rc_r.at[j], core_dev())
        cp.start()
        core_copies.append(cp)

    halo_copies = []
    for ix, iy in halo:
        k = 3 * ix + iy
        cp = copy(hood.at[4], hood.at[k], halo_s.at[k], halo_r.at[k], halo_dev(ix, iy))
        cp.start()
        halo_copies.append(cp)

    x_copies = []
    for d, cp in zip(range(1, XS + 1), core_copies):
        j = lax.rem(x + d, XS)
        cp.wait_recv()
        acc_x[j] = mine[core, j] + recv_c[j]
        if d < XS:
            xc = copy(acc_x.at[j], recv_x.at[x], rx_s.at[j], rx_r.at[x], x_dev(j))
            xc.start()
            x_copies.append(xc)

    fhigh, flow = split(pair_feat)
    fi[...] = jnp.concatenate([fhigh, flow, fhigh], axis=0)
    zrow[...] = jnp.zeros((8, ATOMS), F32)
    zown = pos[2:3] * (1.0 / CUT)
    lane = lax.broadcasted_iota(jnp.int32, (1, ATOMS), 1)
    wrap = NBLK * DEPTH / CUT
    for b in range(NBLK):
        shift = jnp.zeros((1, ATOMS), F32)
        if b + 2 < NBLK:
            shift = jnp.where(lane >= (b + 2) * TILE, -wrap, shift)
        if b >= 2:
            shift = jnp.where(lane < (b - 1) * TILE, wrap, shift)
        zi[b] = zown + shift
    tile_id = lax.broadcasted_iota(jnp.int32, (32, 32), 0)
    for b in range(NBLK):
        found = jnp.where(nbr_ref[b : b + 1, :] == tile_id, 1.0, FAR)
        found = jnp.max(found, axis=1, keepdims=True)
        cmask[:, b * TILE : (b + 1) * TILE] = jnp.broadcast_to(found, (32, TILE))
    acc_p[...] = jnp.zeros((4, 8, ATOMS), F32)
    for cp in halo_copies:
        cp.wait_recv()

    def pair_tile(t, carry):
        k = lax.div(t, NBLK)
        b = lax.rem(t, NBLK)
        cols = pl.ds(pl.multiple_of(b * TILE, TILE), TILE)
        block = hood[k, :, cols]
        high, low = split(block[:PCH])
        fj = jnp.concatenate([high, high, low], axis=0)
        mbuf[...] = lax.dot_general(fj, fi[...], (((0,), (0,)), ((), ())), preferred_element_type=F32)
        shift_x = (lax.div(k, 3) - 1).astype(F32) * (WIDTH / CUT)
        shift_y = (lax.rem(k, 3) - 1).astype(F32) * (WIDTH / CUT)
        which = lax.broadcasted_iota(jnp.int32, (8, TILE), 0)
        shift = jnp.where(which == 0, shift_x, jnp.where(which == 1, shift_y, 0.0))
        pbuf[...] = jnp.transpose(block[PCH:] + shift)
        xi = jnp.broadcast_to(hood[4, PCH : PCH + 1, :], (8, ATOMS))
        yi = jnp.broadcast_to(hood[4, PCH + 1 : PCH + 2, :], (8, ATOMS))
        zz = jnp.broadcast_to(zi[b], (8, ATOMS))
        limit = jnp.broadcast_to(cmask[pl.ds(t, 1), :], (8, ATOMS))
        ax, ay, az, ae = acc_p[0], acc_p[1], acc_p[2], acc_p[3]
        for g in range(TILE // 8):
            pj = pbuf[8 * g : 8 * g + 8, :]
            dx = xi - jnp.broadcast_to(pj[:, 0:1], (8, ATOMS))
            dy = yi - jnp.broadcast_to(pj[:, 1:2], (8, ATOMS))
            dz = zz - jnp.broadcast_to(pj[:, 2:3], (8, ATOMS))
            w = jnp.maximum(limit - (dx * dx + dy * dy + dz * dz), 0.0)
            mw = mbuf[8 * g : 8 * g + 8, :] * w
            ax = ax + mw * dx
            ay = ay + mw * dy
            az = az + mw * dz
            ae = ae + mw * w
        acc_p[0] = ax
        acc_p[1] = ay
        acc_p[2] = az
        acc_p[3] = ae
        return carry

    lax.fori_loop(0, 9 * NBLK, pair_tile, 0)
    force_scale = 4.0 * SCALE / CUT
    for i in range(3):
        fpair[i : i + 1, :] = force_scale * jnp.sum(acc_p[i], axis=0, keepdims=True)
    erow = jnp.sum(acc_p[3], axis=0, keepdims=True)
    own = jnp.sum(pair_feat * pair_feat, axis=0, keepdims=True)
    for b in range(NBLK):
        blk = slice(b * TILE, (b + 1) * TILE)
        named = jnp.maximum(cmask[4 * NBLK + b : 4 * NBLK + b + 1, blk], 0.0)
        fpair[3:4, blk] = erow[:, blk] - named * own[:, blk]
    epart = fpair[3:4, :TILE] + fpair[3:4, TILE : 2 * TILE] + fpair[3:4, 2 * TILE :]
    epart = epart * (0.5 * SCALE)

    for d, cp in enumerate(x_copies):
        j = x_peers[d]
        copy(acc_x.at[j], recv_x.at[j], rx_s.at[j], rx_r.at[j], x_dev(j)).wait_recv()
    recv_x[x] = acc_x[x]
    total = recv_x[0]
    for j in range(1, XS):
        total = total + recv_x[j]
    sum_x[...] = total
    for j in range(ys):
        send_y[j] = sum_x[sub * j : sub * (j + 1), :]
    y_copies = []
    for j in y_peers:
        cp = copy(send_y.at[j], recv_y.at[y], ry_s.at[j], ry_r.at[y], y_dev(j))
        cp.start()
        y_copies.append(cp)

    kx, ky, kz = kidx_ref[0:1, :], kidx_ref[1:2, :], kidx_ref[2:3, :]
    codes[0:1, :] = kx * 17 + ky
    codes[1:2, :] = kz
    coef[...] = jnp.zeros((2, PAIRS, TILE), F32)
    step = 512
    row_id = lax.broadcasted_iota(jnp.int32, (PAIRS, 1), 0)
    tile_of, sub_of = lax.div(row_id, 8), lax.rem(row_id, 8)
    nx = jnp.where(tile_of < 17, sub_of + 1, 0)
    ny = jnp.where(tile_of < 17, tile_of - 8, jnp.where(tile_of == 17, sub_of + 1, 0))
    none = 100000
    code = nx * 17 + ny
    plus = jnp.where((tile_of == 18) & (sub_of > 0), none, code)
    minus = jnp.where(tile_of == 18, none, -code)
    nz_of = lax.rem(lax.broadcasted_iota(jnp.int32, (TILE, 1), 0), 8) + 1

    def count(i, carry):
        cols = pl.ds(pl.multiple_of(i * step, step), step)
        xy, zc = codes[0:1, cols], codes[1:2, cols]
        on_z = jnp.where(zc == nz_of, 1.0, 0.0).astype(BF16)
        for s, target in ((0, plus), (1, minus)):
            on_xy = jnp.where(xy == target, 1.0, 0.0).astype(BF16)
            coef[s] += lax.dot_general(on_xy, on_z, (((1,), (1,)), ((), ())), preferred_element_type=F32)
        return carry

    lax.fori_loop(0, KVEC // step, count, 0)
    two_pi = 2.0 * math.pi
    wx = nx.astype(F32) * (two_pi / (cols_x * WIDTH))
    wy = ny.astype(F32) * (two_pi / (cols_y * WIDTH))
    wz = (lax.rem(lax.broadcasted_iota(jnp.int32, (1, TILE), 1), 8) + 1).astype(F32) * (two_pi / (NBLK * DEPTH))
    ksq = (wx * wx + wy * wy) + wz * wz
    norm = 1.0 / math.sqrt(cols_x * cols_y * ATOMS * KVEC)
    green = 4.0 * norm * jnp.exp(-0.5 * SMEAR * SMEAR * ksq) / ksq
    cplus, cminus = coef[0], coef[1]
    coef[0] = green * (cplus + cminus)
    coef[1] = green * (cplus - cminus)

    for j in y_peers:
        copy(send_y.at[j], recv_y.at[j], ry_s.at[j], ry_r.at[j], y_dev(j)).wait_recv()
    recv_y[y] = send_y[y]
    total = recv_y[0]
    for j in range(1, ys):
        total = total + recv_y[j]

    recv_z[z, 0:sub, :] = total
    recv_z[z, sub : sub + 1, :] = epart
    z_copies = []
    for j in z_peers:
        cp = copy(recv_z.at[z], recv_z.at[z], rz_s.at[j], rz_r.at[z], z_dev(j))
        cp.start()
        z_copies.append(cp)
    for j in z_peers:
        copy(recv_z.at[j], recv_z.at[j], rz_s.at[j], rz_r.at[j], z_dev(j)).wait_recv()
    total = recv_z[0]
    for j in range(1, zs):
        total = total + recv_z[j]
    gath_y[y] = total

    gy_copies = []
    for j in y_peers:
        cp = copy(gath_y.at[y], gath_y.at[y], gy_s.at[j], gy_r.at[y], y_dev(j))
        cp.start()
        gy_copies.append(cp)
    for j in y_peers:
        copy(gath_y.at[j], gath_y.at[j], gy_s.at[j], gy_r.at[j], y_dev(j)).wait_recv()
    esum = gath_y[0, sub : sub + 1, :]
    for j in range(1, ys):
        esum = esum + gath_y[j, sub : sub + 1, :]
    for j in range(ys):
        full[core, x, sub * j : sub * (j + 1), :] = gath_y[j, 0:sub, :]
    full[core, x, PART:, :] = jnp.broadcast_to(esum, (8, TILE))
    gx_copies = []
    for j in x_peers:
        cp = copy(full.at[core, x], full.at[core, x], gx_s.at[j], gx_r.at[x], x_dev(j))
        cp.start()
        gx_copies.append(cp)
    gc_copies = [copy(full.at[core, x], full.at[core, x], gc_s.at[x], gc_r.at[x], core_dev())]
    gc_copies[0].start()
    for j in x_peers:
        copy(full.at[core, j], full.at[core, j], gx_s.at[j], gx_r.at[j], x_dev(j)).wait_recv()
        cp = copy(full.at[core, j], full.at[core, j], gc_s.at[j], gc_r.at[j], core_dev())
        cp.start()
        gc_copies.append(cp)
    for j in range(XS):
        copy(full.at[other, j], full.at[other, j], gc_s.at[j], gc_r.at[j], core_dev()).wait_recv()

    def tile_of_full(half, t):
        return full[half, (8 * t) // PART, (8 * t) % PART : (8 * t) % PART + 8, :]

    sub_id = lax.broadcasted_iota(jnp.int32, (8, TILE), 0).astype(F32) + 1.0
    elong = jnp.zeros((8, TILE), F32)
    for t in range(TILES_C):
        a, b = coef[0, 8 * t : 8 * t + 8, :], coef[1, 8 * t : 8 * t + 8, :]
        cc, cs = tile_of_full(0, t), tile_of_full(1, t)
        if t < TILES_S:
            sc, ss = tile_of_full(0, TILES_C + t), tile_of_full(1, TILES_C + t)
            lcc, lss = a * cc - b * ss, a * ss - b * cc
            lsc, lcs = a * sc + b * cs, a * cs + b * sc
            elong = elong + ((lcc * cc + lss * ss) + (lsc * sc + lcs * cs))
        else:
            lcc, lcs = a * cc, a * cs
            elong = elong + (lcc * cc + lcs * cs)
        rc, rs = row(t), row(TILES_C + t)
        lf[rc, 0:128] = lcc
        lf[rc, 128:256] = lcs
        if t < TILES_S:
            lf[rs, 0:128] = lsc
            lf[rs, 128:256] = lss
            fx = sub_id if t < 17 else None
            fy = float(t - 8) if t < 17 else sub_id
            for base, factor in ((256, fx), (512, fy)):
                if factor is None:
                    lf[rc, base : base + 256] = jnp.zeros((8, 256), F32)
                    lf[rs, base : base + 256] = jnp.zeros((8, 256), F32)
                else:
                    lf[rc, base : base + 128] = factor * lsc
                    lf[rc, base + 128 : base + 256] = factor * lss
                    lf[rs, base : base + 128] = -(factor * lcc)
                    lf[rs, base + 128 : base + 256] = -(factor * lcs)
        else:
            lf[rc, 256:768] = jnp.zeros((8, 512), F32)
    lf[ROWS:, :] = jnp.zeros((PADDED - ROWS, 768), F32)
    high, low = split(lf[...])
    lh[...] = high
    ll[...] = low

    epair = full[0, 0, PART : PART + 1, :]
    for h, j in [(h, j) for h in range(CORES) for j in range(XS)][1:]:
        epair = epair + full[h, j, PART : PART + 1, :]
    etot = 0.5 * jnp.sum(elong, axis=0, keepdims=True) + epair
    energy_ref[0, 0] = jnp.sum(etot) * (1.0 / (cols_x * cols_y * ATOMS))

    vv = (vh[...], vl[...])
    grads = []
    for i in range(3):
        cols = slice(256 * i, 256 * i + 256)
        grads.append(dot3((lh[:, cols], ll[:, cols]), vv, ((0,), (0,))))
    u = uf[...]
    long_x = jnp.sum(u * grads[1], axis=0, keepdims=True)
    long_y = jnp.sum(u * grads[2], axis=0, keepdims=True)
    nz = (lax.rem(lax.broadcasted_iota(jnp.int32, (TILE, 1), 0), 8) + 1).astype(F32)
    curl = (u[:TILE] * grads[0][TILE:] - u[TILE:] * grads[0][:TILE]) * nz
    long_z = jnp.sum(curl, axis=0, keepdims=True)
    force_ref[0:1, :] = fpair[0:1, :] - (two_pi / (cols_x * WIDTH)) * long_x
    force_ref[1:2, :] = fpair[1:2, :] - (two_pi / (cols_y * WIDTH)) * long_y
    force_ref[2:3, :] = fpair[2:3, :] - (two_pi / (NBLK * DEPTH)) * long_z

    for group in (core_copies, halo_copies, x_copies, y_copies, z_copies, gy_copies, gx_copies, gc_copies):
        for cp in group:
            cp.wait_send()


def column(sizes, positions, features, nbr_tiles, kvec_index, weight_charge, weight_pair):
    cols_x, cols_y, ys, z_lo_n, z_hi_n = sizes
    zs = z_lo_n * z_hi_n
    sub = PART // ys
    vmem, dma = pltpu.VMEM, pltpu.SemaphoreType.DMA
    scratch = [
        vmem((9, PCH + 8, ATOMS), F32),
        vmem((CORES, XS, PART, TILE), F32),
        vmem((XS, PART, TILE), F32),
        vmem((XS, PART, TILE), F32),
        vmem((XS, PART, TILE), F32),
        vmem((PART, TILE), F32),
        vmem((ys, sub, TILE), F32),
        vmem((ys, sub, TILE), F32),
        vmem((zs, sub + 1, TILE), F32),
        vmem((ys, sub + 1, TILE), F32),
        vmem((CORES, XS, PART + 8, TILE), F32),
        vmem((PADDED, ATOMS), F32),
        vmem((PADDED, ATOMS), BF16),
        vmem((PADDED, ATOMS), BF16),
        vmem((2 * TILE, ATOMS), F32),
        vmem((2 * TILE, ATOMS), BF16),
        vmem((2 * TILE, ATOMS), BF16),
        vmem((8, ATOMS), F32),
        vmem((PADDED, 768), F32),
        vmem((PADDED, 768), BF16),
        vmem((PADDED, 768), BF16),
        vmem((2, PAIRS, TILE), F32),
        vmem((8, KVEC), jnp.int32),
        vmem((3 * PCH, ATOMS), BF16),
        vmem((NBLK, 1, ATOMS), F32),
        vmem((32, ATOMS), F32),
        vmem((TILE, ATOMS), F32),
        vmem((TILE, 8), F32),
        vmem((4, 8, ATOMS), F32),
        vmem((8, ATOMS), F32),
    ]
    for n in (9, XS, XS, ys, zs, ys, XS, XS):
        scratch += [dma((n,)), dma((n,))]
    whole = pl.BlockSpec(memory_space=pltpu.VMEM)
    energy, forces = pl.pallas_call(
        functools.partial(kernel, sizes),
        out_shape=(
            jax.ShapeDtypeStruct((1, 1), F32),
            jax.ShapeDtypeStruct((3, ATOMS), F32),
        ),
        in_specs=[whole] * 6,
        out_specs=(pl.BlockSpec(memory_space=pltpu.SMEM), whole),
        scratch_shapes=scratch,
        compiler_params=pltpu.CompilerParams(
            collective_id=0, has_side_effects=True, vmem_limit_bytes=40 * 1024 * 1024
        ),
    )(positions[0, 0], features[0, 0], nbr_tiles[0, 0], kvec_index, weight_charge, weight_pair)
    return energy[0, 0], forces[None, None]


def solution(mesh):
    cols_x, cols_y = mesh.shape["gx"], mesh.shape["gy"]
    z_lo_n = 2
    sizes = (cols_x, cols_y, cols_x // z_lo_n, z_lo_n, cols_y // (XS * CORES))
    cell = P("gx", "gy", None, None)
    return jax.shard_map(
        functools.partial(column, sizes),
        mesh=mesh,
        in_specs=(cell, cell, cell, P(), P(), P()),
        out_specs=(P(), cell),
        check_vma=False,
    )
```

```python
import functools
import math

import jax
import jax.numpy as jnp
from jax import lax
from jax.experimental import pallas as pl
from jax.experimental.pallas import tpu as pltpu
from jax.sharding import PartitionSpec as P

WIDTH = 10.0
DEPTH = 12.0
CUT = 5.0
SMEAR = 1.5
SCALE = 0.25
NMAX = 8
TILE = 128
NBLK = 3
ATOMS = NBLK * TILE
QCH = 16
PCH = 16
KVEC = 4096
XS = 4
CORES = 2
TILES_C = 19
TILES_S = 18
ROWS = 8 * (TILES_C + TILES_S)
PAIRS = 8 * TILES_C
PADDED = 320
PART = PADDED // XS
MESH = pl.DeviceIdType.MESH
F32 = jnp.float32
BF16 = jnp.bfloat16
FAR = -1.0e30


def split(value):
    high = value.astype(BF16)
    return high, (value - high.astype(F32)).astype(BF16)


def unit_circle(turns):
    turns = turns - jnp.round(turns)
    half = turns * math.pi
    sq = half * half
    sine = 1.0 / 6227020800.0
    for term in (-1.0 / 39916800.0, 1.0 / 362880.0, -1.0 / 5040.0, 1.0 / 120.0, -1.0 / 6.0, 1.0):
        sine = sine * sq + term
    sine = sine * half
    cosine = 1.0 / 479001600.0
    for term in (-1.0 / 3628800.0, 1.0 / 40320.0, -1.0 / 720.0, 1.0 / 24.0, -0.5, 1.0):
        cosine = cosine * sq + term
    return 1.0 - 2.0 * sine * sine, 2.0 * sine * cosine


def dot3(a, b, dims):
    out = None
    for left, right in ((a[0], b[0]), (a[0], b[1]), (a[1], b[0])):
        term = lax.dot_general(left, right, (dims, ((), ())), preferred_element_type=F32)
        out = term if out is None else out + term
    return out


def kernel(
    sizes,
    pos_hbm,
    feat_hbm,
    nbr_hbm,
    kidx_hbm,
    wc_hbm,
    wp_hbm,
    energy_ref,
    force_ref,
    pos_ref,
    feat_ref,
    nbr_ref,
    kidx_ref,
    wc_ref,
    wp_ref,
    hood,
    mine,
    recv_c,
    acc_x,
    send_p,
    recv_p,
    recv_z,
    gath_p,
    full,
    e_z,
    e_p,
    e_c,
    vf,
    vh,
    vl,
    uf,
    uh,
    ul,
    lf,
    lh,
    ll,
    coef,
    codes,
    fi,
    pi,
    cmask,
    mbuf,
    acc_p,
    acc_e,
    fpair,
    in_s,
    halo_s,
    halo_r,
    rc_s,
    rc_r,
    rp_s,
    rp_r,
    rz_s,
    rz_r,
    gp_s,
    gp_r,
    gc_s,
    gc_r,
    ez_s,
    ez_r,
    ep_s,
    ep_r,
    ec_s,
    ec_r,
):
    cols_x, cols_y, ys, z_lo_n, z_hi_n = sizes
    zs = z_lo_n * z_hi_n
    sub = PART // ys
    gx = lax.axis_index("gx")
    gy = lax.axis_index("gy")
    z_lo, y = lax.div(gx, ys), lax.rem(gx, ys)
    z_hi = lax.div(gy, XS * CORES)
    x = lax.div(lax.rem(gy, XS * CORES), CORES)
    core = lax.rem(gy, CORES)
    z = z_hi * z_lo_n + z_lo
    other = 1 - core
    me = x * ys + y

    inputs = []
    pairs = ((feat_hbm, feat_ref), (wp_hbm, wp_ref), (pos_hbm, pos_ref), (wc_hbm, wc_ref), (nbr_hbm, nbr_ref), (kidx_hbm, kidx_ref))
    for i, (src, dst) in enumerate(pairs):
        cp = pltpu.make_async_copy(src, dst, in_s.at[i])
        cp.start()
        inputs.append(cp)

    core_dev = (gx, gy + 1 - 2 * core)

    def plane_dev(j, k):
        return (z_lo * ys + k, (z_hi * XS + j) * CORES + core)

    def z_dev(j):
        lo, hi = lax.rem(j, z_lo_n), lax.div(j, z_lo_n)
        return (lo * ys + y, (hi * XS + x) * CORES + core)

    def halo_dev(ix, iy):
        return (
            lax.rem(gx + (1 - ix) + cols_x, cols_x),
            lax.rem(gy + (1 - iy) + cols_y, cols_y),
        )

    def around(value, step, size):
        return lax.rem(value + step, size) if step else value

    halo = [(ix, iy) for ix in range(3) for iy in range(3) if (ix, iy) != (1, 1)]
    x_order = [around(x, d, XS) for d in range(XS)]
    y_order = [around(y, d, ys) for d in range(ys)]
    plane = [(j, k) for n, j in enumerate(x_order) for m, k in enumerate(y_order) if n or m]
    z_peers = [around(z, d, zs) for d in range(1, zs)]

    def copy(src, dst, send, recv, dev):
        return pltpu.make_async_remote_copy(
            src_ref=src, dst_ref=dst, send_sem=send, recv_sem=recv, device_id=dev, device_id_type=MESH
        )

    barrier = pltpu.get_barrier_semaphore()
    partners = [core_dev]
    partners += [plane_dev(j, k) for j, k in plane]
    partners += [z_dev(j) for j in z_peers]
    partners += [halo_dev(ix, iy) for ix, iy in halo]
    for dev in partners:
        pl.semaphore_signal(barrier, inc=1, device_id=dev, device_id_type=MESH)

    def landed(ref, sem):
        copy(ref, ref, sem, sem, core_dev).wait_recv()

    def left(ref, sem):
        copy(ref, ref, sem, sem, core_dev).wait_send()


    for cp in inputs[:3]:
        cp.wait()
    feat = feat_ref[...]
    pair_feat = jnp.dot(wp_ref[...], feat, preferred_element_type=F32)
    hood[4, 0:PCH, :] = pair_feat
    hood[4, PCH:, :] = jnp.zeros((8, ATOMS), F32)
    for i in range(3):
        hood[4, PCH + i : PCH + i + 1, :] = pos_ref[i] * (1.0 / CUT)
    pl.semaphore_wait(barrier, len(partners))
    for ix, iy in halo:
        k = 3 * ix + iy
        copy(hood.at[4], hood.at[k], halo_s, halo_r, halo_dev(ix, iy)).start()

    inputs[3].wait()
    charges = jnp.dot(wc_ref[...], feat, preferred_element_type=F32).astype(BF16).astype(F32)
    order = lax.broadcasted_iota(jnp.int32, (8, ATOMS), 0).astype(F32) + 1.0
    gxf, gyf = gx.astype(F32), gy.astype(F32)
    cx, sx = unit_circle(order * ((pos_ref[0] + gxf * WIDTH) * (1.0 / (cols_x * WIDTH))))
    cy, sy = unit_circle(order * ((pos_ref[1] + gyf * WIDTH) * (1.0 / (cols_y * WIDTH))))
    cz, sz = unit_circle(order * (pos_ref[2] * (1.0 / (NBLK * DEPTH))))

    def row(tile):
        return pl.ds(8 * tile, 8)

    for n in range(1, NMAX + 1):
        cyn, syn = cy[n - 1 : n], sy[n - 1 : n]
        cc, ss, sc, cs = cx * cyn, sx * syn, sx * cyn, cx * syn
        vf[row(8 + n), :] = cc - ss
        vf[row(8 - n), :] = cc + ss
        vf[row(TILES_C + 8 + n), :] = sc + cs
        vf[row(TILES_C + 8 - n), :] = sc - cs
    vf[row(8), :] = cx
    vf[row(TILES_C + 8), :] = sx
    vf[row(17), :] = cy
    vf[row(TILES_C + 17), :] = sy
    vf[row(18), :] = jnp.where(order < 1.5, 1.0, 0.0)
    vf[ROWS:, :] = jnp.zeros((PADDED - ROWS, ATOMS), F32)
    for c in range(QCH):
        uf[row(c), :] = cz * charges[c : c + 1]
        uf[row(QCH + c), :] = sz * charges[c : c + 1]
    high, low = split(vf[...])
    vh[...] = high
    vl[...] = low
    high, low = split(uf[...])
    uh[...] = high
    ul[...] = low

    rotated = x_order[1:] + x_order[:1]
    for j in rotated:
        rows = pl.ds(pl.multiple_of(j * PART, PART), PART)
        part = dot3((vh[rows, :], vl[rows, :]), (uh[...], ul[...]), ((1,), (1,)))
        mine[0, j] = part[:, :TILE]
        mine[1, j] = part[:, TILE:]
        copy(mine.at[other, j], recv_c.at[j], rc_s, rc_r.at[j], core_dev).start()

    for j in rotated:
        landed(recv_c.at[j], rc_r.at[j])
        acc_x[...] = mine[core, j] + recv_c[j]
        for k in range(ys):
            send_p[j, k] = acc_x[sub * k : sub * (k + 1), :]
        for m, k in enumerate(y_order):
            if j is x and m == 0:
                recv_p[me] = send_p[x, y]
            else:
                copy(send_p.at[j, k], recv_p.at[me], rp_s, rp_r, plane_dev(j, k)).start()

    fhigh, flow = split(pair_feat)
    stacked = jnp.concatenate([fhigh, flow, fhigh], axis=0).astype(F32)
    fi[...] = jnp.transpose(stacked).astype(BF16)
    own_pos = jnp.transpose(hood[4, PCH:, :])
    for i in range(3):
        pi[i] = jnp.broadcast_to(own_pos[:, i : i + 1], (ATOMS, TILE))
    inputs[4].wait()
    tile_id = lax.broadcasted_iota(jnp.int32, (32, 32), 0)
    for b in range(NBLK):
        found = jnp.where(nbr_ref[b] == tile_id, 1.0, FAR)
        found = jnp.max(found, axis=1, keepdims=True)
        cmask[:, b * TILE : (b + 1) * TILE] = jnp.broadcast_to(found, (32, TILE))
    acc_p[...] = jnp.zeros((3, ATOMS, TILE), F32)
    acc_e[...] = jnp.zeros((32, TILE), F32)
    wrap = NBLK * DEPTH / CUT

    def couple(k, slot):
        high, low = split(hood[k, 0:PCH, :])
        fj = jnp.concatenate([high, high, low], axis=0)
        mbuf[slot] = jnp.dot(fi[...], fj, preferred_element_type=F32)

    def pair_column(k, slot):
        shift_x = (lax.div(k, 3) - 1).astype(F32) * (WIDTH / CUT)
        shift_y = (lax.rem(k, 3) - 1).astype(F32) * (WIDTH / CUT)
        xj = hood[k, PCH : PCH + 1, :] + shift_x
        yj = hood[k, PCH + 1 : PCH + 2, :] + shift_y
        zj = hood[k, PCH + 2 : PCH + 3, :]
        limits = [cmask[pl.ds(NBLK * k + c, 1), :] for c in range(NBLK)]
        ae = acc_e[...]
        for b in range(NBLK):
            for g in range(TILE // 32):
                rows = slice(b * TILE + 32 * g, b * TILE + 32 * g + 32)
                xi, yi, zi = pi[0, rows, :], pi[1, rows, :], pi[2, rows, :]
                ax, ay, az = acc_p[0, rows, :], acc_p[1, rows, :], acc_p[2, rows, :]
                for c in range(NBLK):
                    cols = slice(c * TILE, (c + 1) * TILE)
                    zc = zj[:, cols]
                    if c - b == 2:
                        zc = zc - wrap
                    if b - c == 2:
                        zc = zc + wrap
                    limit = limits[c][:, b * TILE : (b + 1) * TILE]
                    dx, dy, dz = xi - xj[:, cols], yi - yj[:, cols], zi - zc
                    w = jnp.maximum(limit - (dx * dx + dy * dy + dz * dz), 0.0)
                    mw = mbuf[slot, rows, cols] * w
                    ax = ax + mw * dx
                    ay = ay + mw * dy
                    az = az + mw * dz
                    ae = ae + mw * w
                acc_p[0, rows, :] = ax
                acc_p[1, rows, :] = ay
                acc_p[2, rows, :] = az
        acc_e[...] = ae

    couple(4, 0)
    pair_column(jnp.int32(4), 0)

    inputs[5].wait()
    kx, ky, kz = kidx_ref[0:1, :], kidx_ref[1:2, :], kidx_ref[2:3, :]
    codes[0:1, :] = kx * 17 + ky
    codes[1:2, :] = kz
    coef[...] = jnp.zeros((2, PAIRS, TILE), F32)
    step = 512
    row_id = lax.broadcasted_iota(jnp.int32, (PAIRS, 1), 0)
    tile_of, sub_of = lax.div(row_id, 8), lax.rem(row_id, 8)
    nx = jnp.where(tile_of < 17, sub_of + 1, 0)
    ny = jnp.where(tile_of < 17, tile_of - 8, jnp.where(tile_of == 17, sub_of + 1, 0))
    none = 100000
    code = nx * 17 + ny
    plus = jnp.where((tile_of == 18) & (sub_of > 0), none, code)
    minus = jnp.where(tile_of == 18, none, -code)
    nz_of = lax.rem(lax.broadcasted_iota(jnp.int32, (TILE, 1), 0), 8) + 1

    def count(i, carry):
        cols = pl.ds(pl.multiple_of(i * step, step), step)
        xy, zc = codes[0:1, cols], codes[1:2, cols]
        on_z = jnp.where(zc == nz_of, 1.0, 0.0).astype(BF16)
        for s, target in ((0, plus), (1, minus)):
            on_xy = jnp.where(xy == target, 1.0, 0.0).astype(BF16)
            coef[s] += lax.dot_general(on_xy, on_z, (((1,), (1,)), ((), ())), preferred_element_type=F32)
        return carry

    lax.fori_loop(0, KVEC // step, count, 0)
    two_pi = 2.0 * math.pi
    wx = nx.astype(F32) * (two_pi / (cols_x * WIDTH))
    wy = ny.astype(F32) * (two_pi / (cols_y * WIDTH))
    wz = (lax.rem(lax.broadcasted_iota(jnp.int32, (1, TILE), 1), 8) + 1).astype(F32) * (two_pi / (NBLK * DEPTH))
    ksq = (wx * wx + wy * wy) + wz * wz
    norm = 1.0 / math.sqrt(cols_x * cols_y * ATOMS * KVEC)
    green = 4.0 * norm * jnp.exp(-0.5 * SMEAR * SMEAR * ksq) / ksq
    cplus, cminus = coef[0], coef[1]
    coef[0] = green * (cplus + cminus)
    coef[1] = green * (cplus - cminus)

    landed(recv_p.at[1:], rp_r)
    total = recv_p[0]
    for s in range(1, XS * ys):
        total = total + recv_p[s]

    recv_z[z] = total
    for j in z_peers:
        copy(recv_z.at[z], recv_z.at[z], rz_s, rz_r, z_dev(j)).start()

    landed(hood.at[0:8], halo_r)
    couple(5, 1)

    def pair_step(i, carry):
        slot = lax.rem(i, 2)
        couple(lax.rem(i + 5, 9), 1 - slot)
        pair_column(lax.rem(i + 4, 9), slot)
        return carry

    lax.fori_loop(1, 8, pair_step, 0)
    pair_column(jnp.int32(3), 0)
    own = jnp.sum(pair_feat * pair_feat, axis=0, keepdims=True)
    epart = jnp.sum(acc_e[...], axis=0, keepdims=True)
    for b in range(NBLK):
        blk = slice(b * TILE, (b + 1) * TILE)
        named = jnp.maximum(cmask[4 * NBLK + b : 4 * NBLK + b + 1, blk], 0.0)
        epart = epart - named * own[:, blk]
    e_z[z] = epart * (0.5 * SCALE)
    for j in z_peers:
        copy(e_z.at[z], e_z.at[z], ez_s, ez_r, z_dev(j)).start()
    force_scale = 4.0 * SCALE / CUT
    ones = jnp.ones((8, TILE), BF16)
    for i in range(3):
        high, low = split(acc_p[i])
        sums = lax.dot_general(ones, high, (((1,), (1,)), ((), ())), preferred_element_type=F32)
        sums = sums + lax.dot_general(ones, low, (((1,), (1,)), ((), ())), preferred_element_type=F32)
        fpair[i : i + 1, :] = force_scale * sums[0:1]

    landed(recv_z.at[1:], rz_r)
    total = recv_z[0]
    for j in range(1, zs):
        total = total + recv_z[j]

    gath_p[me] = total
    for j, k in plane:
        copy(gath_p.at[me], gath_p.at[me], gp_s, gp_r.at[x], plane_dev(j, k)).start()
    landed(e_z.at[1:], ez_r)
    esum = e_z[0]
    for j in range(1, zs):
        esum = esum + e_z[j]
    e_p[me] = esum
    for j, k in plane:
        copy(e_p.at[me], e_p.at[me], ep_s, ep_r, plane_dev(j, k)).start()
    for j in x_order:
        landed(gath_p.at[pl.ds(j * ys, ys - 1 if j is x else ys)], gp_r.at[j])
        for k in range(ys):
            full[core, j, sub * k : sub * (k + 1), :] = gath_p[j * ys + k]
        copy(full.at[core, j], full.at[core, j], gc_s, gc_r, core_dev).start()
    landed(full.at[other], gc_r)

    def tile_of_full(half, t):
        return full[half, (8 * t) // PART, (8 * t) % PART : (8 * t) % PART + 8, :]

    sub_id = lax.broadcasted_iota(jnp.int32, (8, TILE), 0).astype(F32) + 1.0
    elong = jnp.zeros((8, TILE), F32)
    for t in range(TILES_C):
        a, b = coef[0, 8 * t : 8 * t + 8, :], coef[1, 8 * t : 8 * t + 8, :]
        cc, cs = tile_of_full(0, t), tile_of_full(1, t)
        if t < TILES_S:
            sc, ss = tile_of_full(0, TILES_C + t), tile_of_full(1, TILES_C + t)
            lcc, lss = a * cc - b * ss, a * ss - b * cc
            lsc, lcs = a * sc + b * cs, a * cs + b * sc
            elong = elong + ((lcc * cc + lss * ss) + (lsc * sc + lcs * cs))
        else:
            lcc, lcs = a * cc, a * cs
            elong = elong + (lcc * cc + lcs * cs)
        rc, rs = row(t), row(TILES_C + t)
        lf[rc, 0:128] = lcc
        lf[rc, 128:256] = lcs
        if t < TILES_S:
            lf[rs, 0:128] = lsc
            lf[rs, 128:256] = lss
            fx = sub_id if t < 17 else None
            fy = float(t - 8) if t < 17 else sub_id
            for base, factor in ((256, fx), (512, fy)):
                if factor is None:
                    lf[rc, base : base + 256] = jnp.zeros((8, 256), F32)
                    lf[rs, base : base + 256] = jnp.zeros((8, 256), F32)
                else:
                    lf[rc, base : base + 128] = factor * lsc
                    lf[rc, base + 128 : base + 256] = factor * lss
                    lf[rs, base : base + 128] = -(factor * lcc)
                    lf[rs, base + 128 : base + 256] = -(factor * lcs)
        else:
            lf[rc, 256:768] = jnp.zeros((8, 512), F32)
    lf[ROWS:, :] = jnp.zeros((PADDED - ROWS, 768), F32)
    high, low = split(lf[...])
    lh[...] = high
    ll[...] = low

    vv = (vh[...], vl[...])
    grads = []
    for i in range(3):
        cols = slice(256 * i, 256 * i + 256)
        grads.append(dot3((lh[:, cols], ll[:, cols]), vv, ((0,), (0,))))
    u = uf[...]
    long_x = jnp.sum(u * grads[1], axis=0, keepdims=True)
    long_y = jnp.sum(u * grads[2], axis=0, keepdims=True)
    nz = (lax.rem(lax.broadcasted_iota(jnp.int32, (TILE, 1), 0), 8) + 1).astype(F32)
    curl = (u[:TILE] * grads[0][TILE:] - u[TILE:] * grads[0][:TILE]) * nz
    long_z = jnp.sum(curl, axis=0, keepdims=True)
    force_ref[0] = fpair[0:1, :] - (two_pi / (cols_x * WIDTH)) * long_x
    force_ref[1] = fpair[1:2, :] - (two_pi / (cols_y * WIDTH)) * long_y
    force_ref[2] = fpair[2:3, :] - (two_pi / (NBLK * DEPTH)) * long_z

    landed(e_p.at[1:], ep_r)
    esum = e_p[0]
    for s in range(1, XS * ys):
        esum = esum + e_p[s]
    e_c[core] = esum
    copy(e_c.at[core], e_c.at[core], ec_s, ec_r, core_dev).start()
    landed(e_c.at[other], ec_r)
    etot = 0.5 * jnp.sum(elong, axis=0, keepdims=True) + (e_c[0] + e_c[1])
    energy_ref[0, 0] = jnp.sum(etot) * (1.0 / (cols_x * cols_y * ATOMS))
    left(hood.at[0:8], halo_s)
    left(mine.at[0], rc_s)
    left(recv_p.at[1:], rp_s)
    left(recv_z.at[1:], rz_s)
    left(gath_p.at[1:], gp_s)
    left(full.at[core], gc_s)
    left(e_z.at[1:], ez_s)
    left(e_p.at[1:], ep_s)
    left(e_c.at[core], ec_s)


def column(sizes, positions, features, nbr_tiles, kvec_index, weight_charge, weight_pair):
    cols_x, cols_y, ys, z_lo_n, z_hi_n = sizes
    zs = z_lo_n * z_hi_n
    ps = XS * ys
    sub = PART // ys
    vmem, dma = pltpu.VMEM, pltpu.SemaphoreType.DMA
    scratch = [
        vmem((3, 1, ATOMS), F32),
        vmem((128, ATOMS), BF16),
        vmem((NBLK, 1, 32), jnp.int32),
        vmem((3, KVEC), jnp.int32),
        vmem((QCH, 128), BF16),
        vmem((PCH, 128), BF16),
        vmem((9, PCH + 8, ATOMS), F32),
        vmem((CORES, XS, PART, TILE), F32),
        vmem((XS, PART, TILE), F32),
        vmem((PART, TILE), F32),
        vmem((XS, ys, sub, TILE), F32),
        vmem((ps, sub, TILE), F32),
        vmem((zs, sub, TILE), F32),
        vmem((ps, sub, TILE), F32),
        vmem((CORES, XS, PART, TILE), F32),
        vmem((zs, 1, TILE), F32),
        vmem((ps, 1, TILE), F32),
        vmem((CORES, 1, TILE), F32),
        vmem((PADDED, ATOMS), F32),
        vmem((PADDED, ATOMS), BF16),
        vmem((PADDED, ATOMS), BF16),
        vmem((2 * TILE, ATOMS), F32),
        vmem((2 * TILE, ATOMS), BF16),
        vmem((2 * TILE, ATOMS), BF16),
        vmem((PADDED, 768), F32),
        vmem((PADDED, 768), BF16),
        vmem((PADDED, 768), BF16),
        vmem((2, PAIRS, TILE), F32),
        vmem((8, KVEC), jnp.int32),
        vmem((ATOMS, 3 * PCH), BF16),
        vmem((3, ATOMS, TILE), F32),
        vmem((32, ATOMS), F32),
        vmem((2, ATOMS, ATOMS), F32),
        vmem((3, ATOMS, TILE), F32),
        vmem((32, TILE), F32),
        vmem((8, ATOMS), F32),
        dma((6,)),
    ]
    one, each_x = dma(()), dma((XS,))
    scratch += [one, one, one, each_x, one, one, one, one, one, each_x, one, one, one, one, one, one, one, one]
    anywhere = pl.BlockSpec(memory_space=pl.ANY)
    energy, forces = pl.pallas_call(
        functools.partial(kernel, sizes),
        out_shape=(
            jax.ShapeDtypeStruct((1, 1), F32),
            jax.ShapeDtypeStruct((3, 1, ATOMS), F32),
        ),
        in_specs=[anywhere] * 6,
        out_specs=(pl.BlockSpec(memory_space=pltpu.SMEM), pl.BlockSpec(memory_space=pltpu.VMEM)),
        scratch_shapes=scratch,
        compiler_params=pltpu.CompilerParams(
            collective_id=0, has_side_effects=True, vmem_limit_bytes=60 * 1024 * 1024
        ),
    )(
        positions.reshape(3, 1, ATOMS),
        features[0, 0],
        nbr_tiles.reshape(NBLK, 1, 32),
        kvec_index,
        weight_charge,
        weight_pair,
    )
    return energy[0, 0], forces.reshape(1, 1, 3, ATOMS)


def solution(mesh):
    cols_x, cols_y = mesh.shape["gx"], mesh.shape["gy"]
    z_lo_n = 2
    sizes = (cols_x, cols_y, cols_x // z_lo_n, z_lo_n, cols_y // (XS * CORES))
    cell = P("gx", "gy", None, None)
    return jax.shard_map(
        functools.partial(column, sizes),
        mesh=mesh,
        in_specs=(cell, cell, cell, P(), P(), P()),
        out_specs=(P(), cell),
        check_vma=False,
    )
```

```python
import functools
import math

import jax
import jax.numpy as jnp
from jax import lax
from jax.experimental import pallas as pl
from jax.experimental.pallas import tpu as pltpu
from jax.sharding import PartitionSpec as P

WIDTH = 10.0
DEPTH = 12.0
CUT = 5.0
SMEAR = 1.5
SCALE = 0.25
NMAX = 8
TILE = 128
NBLK = 3
ATOMS = NBLK * TILE
QCH = 16
PCH = 16
KVEC = 4096
XS = 4
CORES = 2
TILES_C = 19
TILES_S = 18
ROWS = 8 * (TILES_C + TILES_S)
PAIRS = 8 * TILES_C
PADDED = 320
PART = PADDED // XS
MESH = pl.DeviceIdType.MESH
F32 = jnp.float32
BF16 = jnp.bfloat16
FAR = -1.0e30


def split(value):
    high = value.astype(BF16)
    return high, (value - high.astype(F32)).astype(BF16)


def unit_circle(turns):
    turns = turns - jnp.round(turns)
    half = turns * math.pi
    sq = half * half
    sine = 1.0 / 6227020800.0
    for term in (-1.0 / 39916800.0, 1.0 / 362880.0, -1.0 / 5040.0, 1.0 / 120.0, -1.0 / 6.0, 1.0):
        sine = sine * sq + term
    sine = sine * half
    cosine = 1.0 / 479001600.0
    for term in (-1.0 / 3628800.0, 1.0 / 40320.0, -1.0 / 720.0, 1.0 / 24.0, -0.5, 1.0):
        cosine = cosine * sq + term
    return 1.0 - 2.0 * sine * sine, 2.0 * sine * cosine


def dot3(a, b, dims):
    out = None
    for left, right in ((a[0], b[0]), (a[0], b[1]), (a[1], b[0])):
        term = lax.dot_general(left, right, (dims, ((), ())), preferred_element_type=F32)
        out = term if out is None else out + term
    return out


def kernel(
    sizes,
    pos_hbm,
    feat_hbm,
    nbr_hbm,
    kidx_hbm,
    wc_hbm,
    wp_hbm,
    energy_ref,
    force_ref,
    pos_ref,
    feat_ref,
    nbr_ref,
    kidx_ref,
    wc_ref,
    wp_ref,
    hood,
    mine,
    recv_c,
    acc_x,
    send_p,
    recv_p,
    recv_z,
    gath_p,
    full,
    e_z,
    e_p,
    e_c,
    vf,
    vh,
    vl,
    uf,
    uh,
    ul,
    lf,
    lh,
    ll,
    coef,
    codes,
    fi,
    pi,
    cmask,
    mbuf,
    acc_p,
    acc_e,
    fpair,
    in_s,
    halo_s,
    halo_r,
    rc_s,
    rc_r,
    rp_s,
    rp_r,
    rz_s,
    rz_r,
    gp_s,
    gp_r,
    gc_s,
    gc_r,
    ez_s,
    ez_r,
    ep_s,
    ep_r,
    ec_s,
    ec_r,
):
    cols_x, cols_y, ys, z_lo_n, z_hi_n = sizes
    zs = z_lo_n * z_hi_n
    sub = PART // ys
    gx = lax.axis_index("gx")
    gy = lax.axis_index("gy")
    z_lo, y = lax.div(gx, ys), lax.rem(gx, ys)
    z_hi = lax.div(gy, XS * CORES)
    x = lax.div(lax.rem(gy, XS * CORES), CORES)
    core = lax.rem(gy, CORES)
    z = z_hi * z_lo_n + z_lo
    other = 1 - core
    me = x * ys + y

    inputs = []
    pairs = ((feat_hbm, feat_ref), (wp_hbm, wp_ref), (pos_hbm, pos_ref), (wc_hbm, wc_ref), (nbr_hbm, nbr_ref), (kidx_hbm, kidx_ref))
    for i, (src, dst) in enumerate(pairs):
        cp = pltpu.make_async_copy(src, dst, in_s.at[i])
        cp.start()
        inputs.append(cp)

    core_dev = (gx, gy + 1 - 2 * core)

    def plane_dev(j, k):
        return (z_lo * ys + k, (z_hi * XS + j) * CORES + core)

    def z_dev(j):
        lo, hi = lax.rem(j, z_lo_n), lax.div(j, z_lo_n)
        return (lo * ys + y, (hi * XS + x) * CORES + core)

    def halo_dev(ix, iy):
        return (
            lax.rem(gx + (1 - ix) + cols_x, cols_x),
            lax.rem(gy + (1 - iy) + cols_y, cols_y),
        )

    def around(value, step, size):
        return lax.rem(value + step, size) if step else value

    halo = [(ix, iy) for ix in range(3) for iy in range(3) if (ix, iy) != (1, 1)]
    x_order = [around(x, d, XS) for d in range(XS)]
    y_order = [around(y, d, ys) for d in range(ys)]
    plane = [(j, k) for n, j in enumerate(x_order) for m, k in enumerate(y_order) if n or m]
    hops = lambda jk: min(jk[0], XS - jk[0]) + min(jk[1], ys - jk[1])
    outward = sorted([(j, k) for j in range(XS) for k in range(ys)], key=hops)
    z_peers = [around(z, d, zs) for d in range(1, zs)]

    def copy(src, dst, send, recv, dev):
        return pltpu.make_async_remote_copy(
            src_ref=src, dst_ref=dst, send_sem=send, recv_sem=recv, device_id=dev, device_id_type=MESH
        )

    barrier = pltpu.get_barrier_semaphore()
    partners = [core_dev]
    partners += [plane_dev(j, k) for j, k in plane]
    partners += [z_dev(j) for j in z_peers]
    partners += [halo_dev(ix, iy) for ix, iy in halo]
    for dev in partners:
        pl.semaphore_signal(barrier, inc=1, device_id=dev, device_id_type=MESH)

    def landed(ref, sem):
        copy(ref, ref, sem, sem, core_dev).wait_recv()

    def left(ref, sem):
        copy(ref, ref, sem, sem, core_dev).wait_send()


    for cp in inputs[:3]:
        cp.wait()
    feat = feat_ref[...]
    pair_feat = jnp.dot(wp_ref[...], feat, preferred_element_type=F32)
    hood[4, 0:PCH, :] = pair_feat
    hood[4, PCH:, :] = jnp.zeros((8, ATOMS), F32)
    for i in range(3):
        hood[4, PCH + i : PCH + i + 1, :] = pos_ref[i] * (1.0 / CUT)
    inputs[3].wait()
    charges = jnp.dot(wc_ref[...], feat, preferred_element_type=F32).astype(BF16).astype(F32)
    order = lax.broadcasted_iota(jnp.int32, (8, ATOMS), 0).astype(F32) + 1.0
    gxf, gyf = gx.astype(F32), gy.astype(F32)
    cx, sx = unit_circle(order * ((pos_ref[0] + gxf * WIDTH) * (1.0 / (cols_x * WIDTH))))
    cy, sy = unit_circle(order * ((pos_ref[1] + gyf * WIDTH) * (1.0 / (cols_y * WIDTH))))
    cz, sz = unit_circle(order * (pos_ref[2] * (1.0 / (NBLK * DEPTH))))

    def row(tile):
        return pl.ds(8 * tile, 8)

    for n in range(1, NMAX + 1):
        cyn, syn = cy[n - 1 : n], sy[n - 1 : n]
        cc, ss, sc, cs = cx * cyn, sx * syn, sx * cyn, cx * syn
        vf[row(8 + n), :] = cc - ss
        vf[row(8 - n), :] = cc + ss
        vf[row(TILES_C + 8 + n), :] = sc + cs
        vf[row(TILES_C + 8 - n), :] = sc - cs
    vf[row(8), :] = cx
    vf[row(TILES_C + 8), :] = sx
    vf[row(17), :] = cy
    vf[row(TILES_C + 17), :] = sy
    vf[row(18), :] = jnp.where(order < 1.5, 1.0, 0.0)
    vf[ROWS:, :] = jnp.zeros((PADDED - ROWS, ATOMS), F32)
    for c in range(QCH):
        uf[row(c), :] = cz * charges[c : c + 1]
        uf[row(QCH + c), :] = sz * charges[c : c + 1]
    high, low = split(vf[...])
    vh[...] = high
    vl[...] = low
    high, low = split(uf[...])
    uh[...] = high
    ul[...] = low

    rotated = [x_order[i] for i in (2, 1, 3, 0)]
    far = [y_order[i] for i in sorted(range(ys), key=lambda i: -min(i, ys - i))]
    for j in rotated:
        rows = pl.ds(pl.multiple_of(j * PART, PART), PART)
        part = lax.dot_general(vh[rows, :], uh[...], (((1,), (1,)), ((), ())), preferred_element_type=F32)
        mine[0, j] = part[:, :TILE]
        mine[1, j] = part[:, TILE:]

    pl.semaphore_wait(barrier, len(partners))
    for j in rotated:
        copy(mine.at[other, j], recv_c.at[j], rc_s, rc_r.at[j], core_dev).start()
    for ix, iy in halo:
        k = 3 * ix + iy
        copy(hood.at[4], hood.at[k], halo_s, halo_r, halo_dev(ix, iy)).start()


    for j in rotated:
        landed(recv_c.at[j], rc_r.at[j])
        acc_x[...] = mine[core, j] + recv_c[j]
        for k in range(ys):
            send_p[j, k] = acc_x[sub * k : sub * (k + 1), :]
        for k in far:
            if j is x and k is y:
                recv_p[me] = send_p[x, y]
            else:
                copy(send_p.at[j, k], recv_p.at[me], rp_s, rp_r, plane_dev(j, k)).start()

    fhigh, flow = split(pair_feat)
    stacked = jnp.concatenate([fhigh, flow, fhigh], axis=0).astype(F32)
    fi[...] = jnp.transpose(stacked).astype(BF16)
    own_pos = jnp.transpose(hood[4, PCH:, :])
    for i in range(3):
        pi[i] = jnp.broadcast_to(own_pos[:, i : i + 1], (ATOMS, TILE))
    inputs[4].wait()
    tile_id = lax.broadcasted_iota(jnp.int32, (32, 32), 0)
    for b in range(NBLK):
        found = jnp.where(nbr_ref[b] == tile_id, 1.0, FAR)
        found = jnp.max(found, axis=1, keepdims=True)
        cmask[:, b * TILE : (b + 1) * TILE] = jnp.broadcast_to(found, (32, TILE))
    acc_p[...] = jnp.zeros((3, ATOMS, TILE), F32)
    acc_e[...] = jnp.zeros((32, TILE), F32)
    wrap = NBLK * DEPTH / CUT

    def couple(k, slot):
        high, low = split(hood[k, 0:PCH, :])
        fj = jnp.concatenate([high, high, low], axis=0)
        mbuf[slot] = jnp.dot(fi[...], fj, preferred_element_type=F32)

    def pair_column(k, slot):
        shift_x = (lax.div(k, 3) - 1).astype(F32) * (WIDTH / CUT)
        shift_y = (lax.rem(k, 3) - 1).astype(F32) * (WIDTH / CUT)
        xj = hood[k, PCH : PCH + 1, :] + shift_x
        yj = hood[k, PCH + 1 : PCH + 2, :] + shift_y
        zj = hood[k, PCH + 2 : PCH + 3, :]
        limits = [cmask[pl.ds(NBLK * k + c, 1), :] for c in range(NBLK)]
        ae = acc_e[...]
        for b in range(NBLK):
            for g in range(TILE // 32):
                rows = slice(b * TILE + 32 * g, b * TILE + 32 * g + 32)
                xi, yi, zi = pi[0, rows, :], pi[1, rows, :], pi[2, rows, :]
                ax, ay, az = acc_p[0, rows, :], acc_p[1, rows, :], acc_p[2, rows, :]
                for c in range(NBLK):
                    cols = slice(c * TILE, (c + 1) * TILE)
                    zc = zj[:, cols]
                    if c - b == 2:
                        zc = zc - wrap
                    if b - c == 2:
                        zc = zc + wrap
                    limit = limits[c][:, b * TILE : (b + 1) * TILE]
                    dx, dy, dz = xi - xj[:, cols], yi - yj[:, cols], zi - zc
                    w = jnp.maximum(limit - (dx * dx + dy * dy + dz * dz), 0.0)
                    mw = mbuf[slot, rows, cols] * w
                    ax = ax + mw * dx
                    ay = ay + mw * dy
                    az = az + mw * dz
                    ae = ae + mw * w
                acc_p[0, rows, :] = ax
                acc_p[1, rows, :] = ay
                acc_p[2, rows, :] = az
        acc_e[...] = ae

    couple(4, 0)
    pair_column(jnp.int32(4), 0)

    inputs[5].wait()
    kx, ky, kz = kidx_ref[0:1, :], kidx_ref[1:2, :], kidx_ref[2:3, :]
    codes[0:1, :] = kx * 17 + ky
    codes[1:2, :] = kz
    coef[...] = jnp.zeros((2, PAIRS, TILE), F32)
    step = 512
    row_id = lax.broadcasted_iota(jnp.int32, (PAIRS, 1), 0)
    tile_of, sub_of = lax.div(row_id, 8), lax.rem(row_id, 8)
    nx = jnp.where(tile_of < 17, sub_of + 1, 0)
    ny = jnp.where(tile_of < 17, tile_of - 8, jnp.where(tile_of == 17, sub_of + 1, 0))
    none = 100000
    code = nx * 17 + ny
    plus = jnp.where((tile_of == 18) & (sub_of > 0), none, code)
    minus = jnp.where(tile_of == 18, none, -code)
    nz_of = lax.rem(lax.broadcasted_iota(jnp.int32, (TILE, 1), 0), 8) + 1

    def count(i, carry):
        cols = pl.ds(pl.multiple_of(i * step, step), step)
        xy, zc = codes[0:1, cols], codes[1:2, cols]
        on_z = jnp.where(zc == nz_of, 1.0, 0.0).astype(BF16)
        for s, target in ((0, plus), (1, minus)):
            on_xy = jnp.where(xy == target, 1.0, 0.0).astype(BF16)
            coef[s] += lax.dot_general(on_xy, on_z, (((1,), (1,)), ((), ())), preferred_element_type=F32)
        return carry

    lax.fori_loop(0, KVEC // step, count, 0)
    two_pi = 2.0 * math.pi
    wx = nx.astype(F32) * (two_pi / (cols_x * WIDTH))
    wy = ny.astype(F32) * (two_pi / (cols_y * WIDTH))
    wz = (lax.rem(lax.broadcasted_iota(jnp.int32, (1, TILE), 1), 8) + 1).astype(F32) * (two_pi / (NBLK * DEPTH))
    ksq = (wx * wx + wy * wy) + wz * wz
    norm = 1.0 / math.sqrt(cols_x * cols_y * ATOMS * KVEC)
    green = 4.0 * norm * jnp.exp(-0.5 * SMEAR * SMEAR * ksq) / ksq
    cplus, cminus = coef[0], coef[1]
    coef[0] = green * (cplus + cminus)
    coef[1] = green * (cplus - cminus)

    landed(hood.at[0:8], halo_r)
    couple(5, 1)

    def pair_step(i, carry):
        slot = lax.rem(i, 2)
        couple(lax.rem(i + 5, 9), 1 - slot)
        pair_column(lax.rem(i + 4, 9), slot)
        return carry

    lax.fori_loop(1, 4, pair_step, 0)

    landed(recv_p.at[1:], rp_r)
    total = recv_p[0]
    for s in range(1, XS * ys):
        total = total + recv_p[s]

    recv_z[z] = total
    for j in sorted(range(zs), key=lambda j: min(j, zs - j)):

        @pl.when(j != z)
        def _(j=j):
            copy(recv_z.at[z], recv_z.at[z], rz_s, rz_r, z_dev(j)).start()


    lax.fori_loop(4, 8, pair_step, 0)
    pair_column(jnp.int32(3), 0)
    own = jnp.sum(pair_feat * pair_feat, axis=0, keepdims=True)
    epart = jnp.sum(acc_e[...], axis=0, keepdims=True)
    for b in range(NBLK):
        blk = slice(b * TILE, (b + 1) * TILE)
        named = jnp.maximum(cmask[4 * NBLK + b : 4 * NBLK + b + 1, blk], 0.0)
        epart = epart - named * own[:, blk]
    e_c[core] = epart * (0.5 * SCALE)
    copy(e_c.at[core], e_c.at[core], ec_s, ec_r, core_dev).start()
    force_scale = 4.0 * SCALE / CUT
    ones = jnp.ones((8, TILE), BF16)
    for i in range(3):
        high, low = split(acc_p[i])
        sums = lax.dot_general(ones, high, (((1,), (1,)), ((), ())), preferred_element_type=F32)
        sums = sums + lax.dot_general(ones, low, (((1,), (1,)), ((), ())), preferred_element_type=F32)
        fpair[i : i + 1, :] = force_scale * sums[0:1]

    landed(e_c.at[other], ec_r)
    e_z[z] = e_c[0] + e_c[1]
    for j in z_peers:
        copy(e_z.at[z], e_z.at[z], ez_s, ez_r, z_dev(j)).start()

    landed(recv_z.at[1:], rz_r)
    total = recv_z[0]
    for j in range(1, zs):
        total = total + recv_z[j]

    gath_p[me] = total
    for j, k in outward:

        @pl.when(j * ys + k != me)
        def _(j=j, k=k):
            copy(gath_p.at[me], gath_p.at[me], gp_s, gp_r.at[x], plane_dev(j, k)).start()

    landed(e_z.at[1:], ez_r)
    esum = e_z[0]
    for j in range(1, zs):
        esum = esum + e_z[j]
    e_p[me] = esum
    for j, k in plane:
        copy(e_p.at[me], e_p.at[me], ep_s, ep_r, plane_dev(j, k)).start()
    for j in x_order:
        landed(gath_p.at[pl.ds(j * ys, ys - 1 if j is x else ys)], gp_r.at[j])
        for k in range(ys):
            full[core, j, sub * k : sub * (k + 1), :] = gath_p[j * ys + k]
        copy(full.at[core, j], full.at[core, j], gc_s, gc_r, core_dev).start()
    landed(full.at[other], gc_r)

    def tile_of_full(half, t):
        return full[half, (8 * t) // PART, (8 * t) % PART : (8 * t) % PART + 8, :]

    sub_id = lax.broadcasted_iota(jnp.int32, (8, TILE), 0).astype(F32) + 1.0
    elong = jnp.zeros((8, TILE), F32)
    for t in range(TILES_C):
        a, b = coef[0, 8 * t : 8 * t + 8, :], coef[1, 8 * t : 8 * t + 8, :]
        cc, cs = tile_of_full(0, t), tile_of_full(1, t)
        if t < TILES_S:
            sc, ss = tile_of_full(0, TILES_C + t), tile_of_full(1, TILES_C + t)
            lcc, lss = a * cc - b * ss, a * ss - b * cc
            lsc, lcs = a * sc + b * cs, a * cs + b * sc
            elong = elong + ((lcc * cc + lss * ss) + (lsc * sc + lcs * cs))
        else:
            lcc, lcs = a * cc, a * cs
            elong = elong + (lcc * cc + lcs * cs)
        rc, rs = row(t), row(TILES_C + t)
        lf[rc, 0:128] = lcc
        lf[rc, 128:256] = lcs
        if t < TILES_S:
            lf[rs, 0:128] = lsc
            lf[rs, 128:256] = lss
            fx = sub_id if t < 17 else None
            fy = float(t - 8) if t < 17 else sub_id
            for base, factor in ((256, fx), (512, fy)):
                if factor is None:
                    lf[rc, base : base + 256] = jnp.zeros((8, 256), F32)
                    lf[rs, base : base + 256] = jnp.zeros((8, 256), F32)
                else:
                    lf[rc, base : base + 128] = factor * lsc
                    lf[rc, base + 128 : base + 256] = factor * lss
                    lf[rs, base : base + 128] = -(factor * lcc)
                    lf[rs, base + 128 : base + 256] = -(factor * lcs)
        else:
            lf[rc, 256:768] = jnp.zeros((8, 512), F32)
    lf[ROWS:, :] = jnp.zeros((PADDED - ROWS, 768), F32)
    lh[...] = lf[...].astype(BF16)

    vv = (vh[...], vl[...])
    grads = []
    for i in range(3):
        cols = slice(256 * i, 256 * i + 256)
        grads.append(lax.dot_general(lh[:, cols], vv[0], (((0,), (0,)), ((), ())), preferred_element_type=F32))
    u = uf[...]
    long_x = jnp.sum(u * grads[1], axis=0, keepdims=True)
    long_y = jnp.sum(u * grads[2], axis=0, keepdims=True)
    nz = (lax.rem(lax.broadcasted_iota(jnp.int32, (TILE, 1), 0), 8) + 1).astype(F32)
    curl = (u[:TILE] * grads[0][TILE:] - u[TILE:] * grads[0][:TILE]) * nz
    long_z = jnp.sum(curl, axis=0, keepdims=True)
    force_ref[0] = fpair[0:1, :] - (two_pi / (cols_x * WIDTH)) * long_x
    force_ref[1] = fpair[1:2, :] - (two_pi / (cols_y * WIDTH)) * long_y
    force_ref[2] = fpair[2:3, :] - (two_pi / (NBLK * DEPTH)) * long_z

    landed(e_p.at[1:], ep_r)
    esum = e_p[0]
    for s in range(1, XS * ys):
        esum = esum + e_p[s]
    etot = 0.5 * jnp.sum(elong, axis=0, keepdims=True) + esum
    energy_ref[0, 0] = jnp.sum(etot) * (1.0 / (cols_x * cols_y * ATOMS))
    left(hood.at[0:8], halo_s)
    left(mine.at[0], rc_s)
    left(recv_p.at[1:], rp_s)
    left(recv_z.at[1:], rz_s)
    left(gath_p.at[1:], gp_s)
    left(full.at[core], gc_s)
    left(e_z.at[1:], ez_s)
    left(e_p.at[1:], ep_s)
    left(e_c.at[core], ec_s)


def column(sizes, positions, features, nbr_tiles, kvec_index, weight_charge, weight_pair):
    cols_x, cols_y, ys, z_lo_n, z_hi_n = sizes
    zs = z_lo_n * z_hi_n
    ps = XS * ys
    sub = PART // ys
    vmem, dma = pltpu.VMEM, pltpu.SemaphoreType.DMA
    scratch = [
        vmem((3, 1, ATOMS), F32),
        vmem((128, ATOMS), BF16),
        vmem((NBLK, 1, 32), jnp.int32),
        vmem((3, KVEC), jnp.int32),
        vmem((QCH, 128), BF16),
        vmem((PCH, 128), BF16),
        vmem((9, PCH + 8, ATOMS), F32),
        vmem((CORES, XS, PART, TILE), F32),
        vmem((XS, PART, TILE), F32),
        vmem((PART, TILE), F32),
        vmem((XS, ys, sub, TILE), F32),
        vmem((ps, sub, TILE), F32),
        vmem((zs, sub, TILE), F32),
        vmem((ps, sub, TILE), F32),
        vmem((CORES, XS, PART, TILE), F32),
        vmem((zs, 1, TILE), F32),
        vmem((ps, 1, TILE), F32),
        vmem((CORES, 1, TILE), F32),
        vmem((PADDED, ATOMS), F32),
        vmem((PADDED, ATOMS), BF16),
        vmem((PADDED, ATOMS), BF16),
        vmem((2 * TILE, ATOMS), F32),
        vmem((2 * TILE, ATOMS), BF16),
        vmem((2 * TILE, ATOMS), BF16),
        vmem((PADDED, 768), F32),
        vmem((PADDED, 768), BF16),
        vmem((PADDED, 768), BF16),
        vmem((2, PAIRS, TILE), F32),
        vmem((8, KVEC), jnp.int32),
        vmem((ATOMS, 3 * PCH), BF16),
        vmem((3, ATOMS, TILE), F32),
        vmem((32, ATOMS), F32),
        vmem((2, ATOMS, ATOMS), F32),
        vmem((3, ATOMS, TILE), F32),
        vmem((32, TILE), F32),
        vmem((8, ATOMS), F32),
        dma((6,)),
    ]
    one, each_x = dma(()), dma((XS,))
    scratch += [one, one, one, each_x, one, one, one, one, one, each_x, one, one, one, one, one, one, one, one]
    anywhere = pl.BlockSpec(memory_space=pl.ANY)
    energy, forces = pl.pallas_call(
        functools.partial(kernel, sizes),
        out_shape=(
            jax.ShapeDtypeStruct((1, 1), F32),
            pltpu.VMEM((3, 1, ATOMS), F32),
        ),
        in_specs=[anywhere] * 6,
        out_specs=(pl.BlockSpec(memory_space=pltpu.SMEM), pl.BlockSpec(memory_space=pltpu.VMEM)),
        scratch_shapes=scratch,
        compiler_params=pltpu.CompilerParams(
            collective_id=0, has_side_effects=True, vmem_limit_bytes=60 * 1024 * 1024
        ),
    )(
        positions.reshape(3, 1, ATOMS),
        features[0, 0],
        nbr_tiles.reshape(NBLK, 1, 32),
        kvec_index,
        weight_charge,
        weight_pair,
    )
    return energy[0, 0], forces.reshape(1, 1, 3, ATOMS)


def solution(mesh):
    cols_x, cols_y = mesh.shape["gx"], mesh.shape["gy"]
    z_lo_n = 2
    sizes = (cols_x, cols_y, cols_x // z_lo_n, z_lo_n, cols_y // (XS * CORES))
    cell = P("gx", "gy", None, None)
    return jax.shard_map(
        functools.partial(column, sizes),
        mesh=mesh,
        in_specs=(cell, cell, cell, P(), P(), P()),
        out_specs=(P(), cell),
        check_vma=False,
    )
```

```python
import functools
import math

import jax
import jax.numpy as jnp
from jax import lax
from jax.experimental import pallas as pl
from jax.experimental.pallas import tpu as pltpu
from jax.sharding import PartitionSpec as P

WIDTH = 10.0
DEPTH = 12.0
CUT = 5.0
SMEAR = 1.5
SCALE = 0.25
NMAX = 8
TILE = 128
NBLK = 3
ATOMS = NBLK * TILE
QCH = 16
PCH = 16
KVEC = 4096
XS = 4
CORES = 2
TILES_C = 19
TILES_S = 18
ROWS = 8 * (TILES_C + TILES_S)
PAIRS = 8 * TILES_C
PADDED = 320
PART = PADDED // XS
MESH = pl.DeviceIdType.MESH
F32 = jnp.float32
BF16 = jnp.bfloat16
FAR = -1.0e30


def split(value):
    high = value.astype(BF16)
    return high, (value - high.astype(F32)).astype(BF16)


def unit_circle(turns):
    turns = turns - jnp.round(turns)
    half = turns * math.pi
    sq = half * half
    sine = 1.0 / 6227020800.0
    for term in (-1.0 / 39916800.0, 1.0 / 362880.0, -1.0 / 5040.0, 1.0 / 120.0, -1.0 / 6.0, 1.0):
        sine = sine * sq + term
    sine = sine * half
    cosine = 1.0 / 479001600.0
    for term in (-1.0 / 3628800.0, 1.0 / 40320.0, -1.0 / 720.0, 1.0 / 24.0, -0.5, 1.0):
        cosine = cosine * sq + term
    return 1.0 - 2.0 * sine * sine, 2.0 * sine * cosine


def kernel(
    sizes,
    pos_hbm,
    feat_hbm,
    nbr_hbm,
    kidx_hbm,
    wc_hbm,
    wp_hbm,
    out_ref,
    pos_ref,
    feat_ref,
    nbr_ref,
    kidx_ref,
    wc_ref,
    wp_ref,
    hood,
    mine,
    recv_c,
    acc_x,
    send_p,
    recv_p,
    recv_z,
    gath_p,
    full,
    e_z,
    e_p,
    vf,
    vh,
    uf,
    uh,
    lf,
    coef,
    codes,
    fi,
    pi,
    cmask,
    mbuf,
    acc_p,
    acc_e,
    fpair,
    in_s,
    halo_s,
    halo_x,
    halo_y,
    halo_d,
    rc_s,
    rc_r,
    rp_s,
    rp_r,
    rz_s,
    rz_r,
    gp_s,
    gp_r,
    gc_s,
    gc_r,
    ez_s,
    ez_r,
    ep_s,
    ep_r,
):
    cols_x, cols_y, ys, z_lo_n, z_hi_n = sizes
    zs = z_lo_n * z_hi_n
    sub = PART // ys
    gx = lax.axis_index("gx")
    gy = lax.axis_index("gy")
    z_lo, y = lax.div(gx, ys), lax.rem(gx, ys)
    z_hi = lax.div(gy, XS * CORES)
    x = lax.div(lax.rem(gy, XS * CORES), CORES)
    core = lax.rem(gy, CORES)
    z = z_hi * z_lo_n + z_lo
    other = 1 - core
    me = x * ys + y

    inputs = []
    pairs = ((feat_hbm, feat_ref), (wp_hbm, wp_ref), (pos_hbm, pos_ref), (wc_hbm, wc_ref), (nbr_hbm, nbr_ref), (kidx_hbm, kidx_ref))
    for i, (src, dst) in enumerate(pairs):
        cp = pltpu.make_async_copy(src, dst, in_s.at[i])
        cp.start()
        inputs.append(cp)

    core_dev = (gx, gy + 1 - 2 * core)

    def plane_dev(j, k):
        return (z_lo * ys + k, (z_hi * XS + j) * CORES + core)

    def z_dev(j, core=core):
        lo, hi = lax.rem(j, z_lo_n), lax.div(j, z_lo_n)
        return (lo * ys + y, (hi * XS + x) * CORES + core)

    def halo_dev(ix, iy):
        return (
            lax.rem(gx + (1 - ix) + cols_x, cols_x),
            lax.rem(gy + (1 - iy) + cols_y, cols_y),
        )

    def around(value, step, size):
        return lax.rem(value + step, size) if step else value

    halo = [(0, 1), (2, 1), (1, 0), (1, 2)]
    x_order = [around(x, d, XS) for d in range(XS)]
    y_order = [around(y, d, ys) for d in range(ys)]
    plane = [(j, k) for n, j in enumerate(x_order) for m, k in enumerate(y_order) if n or m]
    hops = lambda jk: min(jk[0], XS - jk[0]) + min(jk[1], ys - jk[1])
    outward = sorted([(j, k) for j in range(XS) for k in range(ys)], key=hops)
    z_peers = [around(z, d, zs) for d in range(1, zs)]

    def copy(src, dst, send, recv, dev):
        return pltpu.make_async_remote_copy(
            src_ref=src, dst_ref=dst, send_sem=send, recv_sem=recv, device_id=dev, device_id_type=MESH
        )

    barrier = pltpu.get_barrier_semaphore()
    steps = [(n, m) for n in range(XS) for m in range(ys) if n or m]
    steps = sorted(steps, key=lambda nm: -(min(nm[0], XS - nm[0]) + min(nm[1], ys - nm[1])))
    partners = [plane_dev(x_order[n], y_order[m]) for n, m in steps]
    partners += [z_dev(z_peers[d - 1]) for d in sorted(range(1, zs), key=lambda d: -min(d, zs - d))]
    partners += [z_dev(j, other) for j in z_peers]
    partners += [core_dev]
    partners += [halo_dev(ix, iy) for ix, iy in halo]
    for dev in partners:
        pl.semaphore_signal(barrier, inc=1, device_id=dev, device_id_type=MESH)

    def landed(ref, sem):
        copy(ref, ref, sem, sem, core_dev).wait_recv()

    def left(ref, sem):
        copy(ref, ref, sem, sem, core_dev).wait_send()


    for cp in inputs[:3]:
        cp.wait()
    feat = feat_ref[...]
    pair_feat = jnp.dot(wp_ref[...], feat, preferred_element_type=F32)
    hood[4, 0:PCH, :] = pair_feat
    for i in range(3):
        hood[4, PCH + i : PCH + i + 1, :] = pos_ref[i] * (1.0 / CUT)
    inputs[3].wait()
    charges = jnp.dot(wc_ref[...], feat, preferred_element_type=F32).astype(BF16).astype(F32)
    order = lax.broadcasted_iota(jnp.int32, (8, ATOMS), 0).astype(F32) + 1.0
    gxf, gyf = gx.astype(F32), gy.astype(F32)
    cx, sx = unit_circle(order * ((pos_ref[0] + gxf * WIDTH) * (1.0 / (cols_x * WIDTH))))
    cy, sy = unit_circle(order * ((pos_ref[1] + gyf * WIDTH) * (1.0 / (cols_y * WIDTH))))
    cz, sz = unit_circle(order * (pos_ref[2] * (1.0 / (NBLK * DEPTH))))

    def row(tile):
        return pl.ds(8 * tile, 8)

    for n in range(1, NMAX + 1):
        cyn, syn = cy[n - 1 : n], sy[n - 1 : n]
        cc, ss, sc, cs = cx * cyn, sx * syn, sx * cyn, cx * syn
        vf[row(8 + n), :] = cc - ss
        vf[row(8 - n), :] = cc + ss
        vf[row(TILES_C + 8 + n), :] = sc + cs
        vf[row(TILES_C + 8 - n), :] = sc - cs
    vf[row(8), :] = cx
    vf[row(TILES_C + 8), :] = sx
    vf[row(17), :] = cy
    vf[row(TILES_C + 17), :] = sy
    vf[row(18), :] = jnp.where(order < 1.5, 1.0, 0.0)
    vf[ROWS:, :] = jnp.zeros((PADDED - ROWS, ATOMS), F32)
    for c in range(QCH):
        h, first = c // 8, 8 * (c % 8)
        uf[h, first : first + 8, :] = cz * charges[c : c + 1]
        uf[h, 64 + first : 72 + first, :] = sz * charges[c : c + 1]
    vh[...] = vf[...].astype(BF16)
    uh[...] = uf[...].reshape(2 * TILE, ATOMS).astype(BF16)

    rotated = [x_order[i] for i in (2, 1, 3, 0)]
    far = [y_order[i] for i in sorted(range(ys), key=lambda i: -min(i, ys - i))]
    for j in rotated:
        rows = pl.ds(pl.multiple_of(j * PART, PART), PART)
        part = lax.dot_general(vh[rows, :], uh[...], (((1,), (1,)), ((), ())), preferred_element_type=F32)
        mine[0, j] = part[:, :TILE]
        mine[1, j] = part[:, TILE:]

    pl.semaphore_wait(barrier, len(partners))
    for j in rotated:
        copy(mine.at[other, j], recv_c.at[j], rc_s, rc_r.at[j], core_dev).start()
    for ix, iy in halo:
        k = 3 * ix + iy
        copy(hood.at[4], hood.at[k], halo_s, halo_x if iy == 1 else halo_y, halo_dev(ix, iy)).start()


    for j in rotated:
        landed(recv_c.at[j], rc_r.at[j])
        acc_x[...] = mine[core, j] + recv_c[j]
        for k in range(ys):
            send_p[j, k] = acc_x[sub * k : sub * (k + 1), :]
        for k in far:
            if j is x and k is y:
                recv_p[me] = send_p[x, y]
            else:
                copy(send_p.at[j, k], recv_p.at[me], rp_s, rp_r, plane_dev(j, k)).start()

    fhigh, flow = split(pair_feat)
    stacked = jnp.concatenate([fhigh, flow, fhigh], axis=0).astype(F32)
    fi[...] = jnp.transpose(stacked).astype(BF16)
    own_pos = [pos_ref[i] * (1.0 / CUT) for i in range(3)] + [jnp.zeros((5, ATOMS), F32)]
    own_pos = jnp.transpose(jnp.concatenate(own_pos, axis=0))
    for i in range(3):
        pi[i] = jnp.broadcast_to(own_pos[:, i : i + 1], (ATOMS, TILE))
    inputs[4].wait()
    tile_id = lax.broadcasted_iota(jnp.int32, (32, 32), 0)
    for b in range(NBLK):
        found = jnp.where(nbr_ref[b] == tile_id, 1.0, FAR)
        found = jnp.max(found, axis=1, keepdims=True)
        cmask[:, b * TILE : (b + 1) * TILE] = jnp.broadcast_to(found, (32, TILE))
    acc_p[...] = jnp.zeros((3, ATOMS, TILE), F32)
    acc_e[...] = jnp.zeros((32, TILE), F32)
    wrap = NBLK * DEPTH / CUT

    def couple(k, slot):
        high, low = split(hood[k, 0:PCH, :])
        fj = jnp.concatenate([high, high, low], axis=0)
        mbuf[slot] = jnp.dot(fi[...], fj, preferred_element_type=F32)

    def pair_column(k, slot):
        shift_x = (lax.div(k, 3) - 1).astype(F32) * (WIDTH / CUT)
        shift_y = (lax.rem(k, 3) - 1).astype(F32) * (WIDTH / CUT)
        xj = hood[k, PCH : PCH + 1, :] + shift_x
        yj = hood[k, PCH + 1 : PCH + 2, :] + shift_y
        zj = hood[k, PCH + 2 : PCH + 3, :]
        limits = [cmask[pl.ds(NBLK * k + c, 1), :] for c in range(NBLK)]
        ae = acc_e[...]
        for b in range(NBLK):
            for g in range(TILE // 32):
                rows = slice(b * TILE + 32 * g, b * TILE + 32 * g + 32)
                xi, yi, zi = pi[0, rows, :], pi[1, rows, :], pi[2, rows, :]
                ax, ay, az = acc_p[0, rows, :], acc_p[1, rows, :], acc_p[2, rows, :]
                for c in range(NBLK):
                    cols = slice(c * TILE, (c + 1) * TILE)
                    zc = zj[:, cols]
                    if c - b == 2:
                        zc = zc - wrap
                    if b - c == 2:
                        zc = zc + wrap
                    limit = limits[c][:, b * TILE : (b + 1) * TILE]
                    dx, dy, dz = xi - xj[:, cols], yi - yj[:, cols], zi - zc
                    w = jnp.maximum(limit - (dx * dx + dy * dy + dz * dz), 0.0)
                    mw = mbuf[slot, rows, cols] * w
                    ax = ax + mw * dx
                    ay = ay + mw * dy
                    az = az + mw * dz
                    ae = ae + mw * w
                acc_p[0, rows, :] = ax
                acc_p[1, rows, :] = ay
                acc_p[2, rows, :] = az
        acc_e[...] = ae

    couple(4, 0)
    pair_column(jnp.int32(4), 0)

    landed(hood.at[0:2], halo_x)
    for ix in (0, 2):
        for iy in (0, 2):
            copy(hood.at[3 * ix + 1], hood.at[3 * ix + iy], halo_s, halo_d, halo_dev(1, iy)).start()
    landed(hood.at[0:2], halo_y)

    def pair_columns(column_of):
        couple(column_of(0), 0)

        def pair_step(i, carry):
            slot = lax.rem(i, 2)
            couple(column_of(i + 1), 1 - slot)
            pair_column(column_of(i), slot)
            return carry

        lax.fori_loop(0, 3, pair_step, 0)
        pair_column(jnp.int32(column_of(3)), 1)

    pair_columns(lambda i: 2 * i + 1)

    landed(recv_p.at[1:], rp_r)
    total = recv_p[0]
    for s in range(1, XS * ys):
        total = total + recv_p[s]

    recv_z[z] = total
    for j in sorted(range(zs), key=lambda j: min(j, zs - j)):

        @pl.when(j != z)
        def _(j=j):
            copy(recv_z.at[z], recv_z.at[z], rz_s, rz_r, z_dev(j)).start()


    landed(hood.at[0:4], halo_d)
    pair_columns(lambda i: 2 * i + 2 * (i // 2) if isinstance(i, int) else 2 * i + 2 * lax.div(i, 2))
    own = jnp.sum(pair_feat * pair_feat, axis=0, keepdims=True)
    epart = jnp.sum(acc_e[...], axis=0, keepdims=True)
    for b in range(NBLK):
        blk = slice(b * TILE, (b + 1) * TILE)
        named = jnp.maximum(cmask[4 * NBLK + b : 4 * NBLK + b + 1, blk], 0.0)
        epart = epart - named * own[:, blk]
    part = z * CORES + core
    e_z[part] = epart * (0.5 * SCALE)
    for j in z_peers:
        copy(e_z.at[part], e_z.at[part], ez_s, ez_r, z_dev(j)).start()
        copy(e_z.at[part], e_z.at[part], ez_s, ez_r, z_dev(j, other)).start()
    copy(e_z.at[part], e_z.at[part], ez_s, ez_r, core_dev).start()
    force_scale = 4.0 * SCALE / CUT
    ones = jnp.ones((8, TILE), BF16)
    for i in range(3):
        high, low = split(acc_p[i])
        sums = lax.dot_general(ones, high, (((1,), (1,)), ((), ())), preferred_element_type=F32)
        sums = sums + lax.dot_general(ones, low, (((1,), (1,)), ((), ())), preferred_element_type=F32)
        fpair[i : i + 1, :] = force_scale * sums[0:1]

    landed(recv_z.at[1:], rz_r)
    total = recv_z[0]
    for j in range(1, zs):
        total = total + recv_z[j]

    gath_p[me] = total
    for j, k in outward:

        @pl.when(j * ys + k != me)
        def _(j=j, k=k):
            copy(gath_p.at[me], gath_p.at[me], gp_s, gp_r.at[x], plane_dev(j, k)).start()

    landed(e_z.at[1:], ez_r)
    esum = e_z[0]
    for j in range(1, CORES * zs):
        esum = esum + e_z[j]
    e_p[me] = esum
    for j, k in plane:
        copy(e_p.at[me], e_p.at[me], ep_s, ep_r, plane_dev(j, k)).start()
    inputs[5].wait()
    kx, ky, kz = kidx_ref[0:1, :], kidx_ref[1:2, :], kidx_ref[2:3, :]
    codes[0:1, :] = kx * 17 + ky
    codes[1:2, :] = kz
    coef[...] = jnp.zeros((2, PAIRS, TILE), F32)
    step = 512
    row_id = lax.broadcasted_iota(jnp.int32, (PAIRS, 1), 0)
    tile_of, sub_of = lax.div(row_id, 8), lax.rem(row_id, 8)
    nx = jnp.where(tile_of < 17, sub_of + 1, 0)
    ny = jnp.where(tile_of < 17, tile_of - 8, jnp.where(tile_of == 17, sub_of + 1, 0))
    none = 100000
    code = nx * 17 + ny
    plus = jnp.where((tile_of == 18) & (sub_of > 0), none, code)
    minus = jnp.where(tile_of == 18, none, -code)
    nz_of = lax.rem(lax.broadcasted_iota(jnp.int32, (TILE, 1), 0), 8) + 1

    def count(i, carry):
        cols = pl.ds(pl.multiple_of(i * step, step), step)
        xy, zc = codes[0:1, cols], codes[1:2, cols]
        on_z = jnp.where(zc == nz_of, 1.0, 0.0).astype(BF16)
        for s, target in ((0, plus), (1, minus)):
            on_xy = jnp.where(xy == target, 1.0, 0.0).astype(BF16)
            coef[s] += lax.dot_general(on_xy, on_z, (((1,), (1,)), ((), ())), preferred_element_type=F32)
        return carry

    lax.fori_loop(0, KVEC // step, count, 0)
    two_pi = 2.0 * math.pi
    wx = nx.astype(F32) * (two_pi / (cols_x * WIDTH))
    wy = ny.astype(F32) * (two_pi / (cols_y * WIDTH))
    wz = (lax.rem(lax.broadcasted_iota(jnp.int32, (1, TILE), 1), 8) + 1).astype(F32) * (two_pi / (NBLK * DEPTH))
    ksq = (wx * wx + wy * wy) + wz * wz
    norm = 1.0 / math.sqrt(cols_x * cols_y * ATOMS * KVEC)
    green = 4.0 * norm * jnp.exp(-0.5 * SMEAR * SMEAR * ksq) / ksq
    cplus, cminus = coef[0], coef[1]
    coef[0] = green * (cplus + cminus)
    lanes = lax.broadcasted_iota(jnp.int32, (1, TILE), 1)
    coef[1] = jnp.where(lanes < 64, -green, green) * (cplus - cminus)

    for j in x_order:
        landed(gath_p.at[pl.ds(j * ys, ys - 1 if j is x else ys)], gp_r.at[j])
        for k in range(ys):
            full[core, j, sub * k : sub * (k + 1), :] = gath_p[j * ys + k]
        copy(full.at[core, j], full.at[core, j], gc_s, gc_r, core_dev).start()
    sub_id = lax.broadcasted_iota(jnp.int32, (8, TILE), 0).astype(F32) + 1.0
    nz = (lax.rem(lax.broadcasted_iota(jnp.int32, (64, 1), 0), 8) + 1).astype(F32)

    def field(h):
        def tile_of(t):
            return full[h, (8 * t) // PART, (8 * t) % PART : (8 * t) % PART + 8, :]

        elong = jnp.zeros((8, TILE), F32)
        for t in range(TILES_C):
            a, b = coef[0, 8 * t : 8 * t + 8, :], coef[1, 8 * t : 8 * t + 8, :]
            rc, rs = row(t), row(TILES_C + t)
            xc = tile_of(t)
            if t == TILES_S:
                lc = a * xc
                elong = elong + lc * xc
                lf[rc, 0:TILE] = lc
                lf[rc, TILE:] = jnp.zeros((8, 2 * TILE), F32)
                continue
            xs = tile_of(TILES_C + t)
            lc = a * xc + b * pltpu.roll(xs, 64, 1)
            ls = a * xs - b * pltpu.roll(xc, 64, 1)
            elong = elong + (lc * xc + ls * xs)
            lf[rc, 0:TILE] = lc
            lf[rs, 0:TILE] = ls
            fx = sub_id if t < 17 else 0.0
            fy = float(t - 8) if t < 17 else sub_id
            for base, factor in ((TILE, fx), (2 * TILE, fy)):
                lf[rc, base : base + TILE] = factor * ls
                lf[rs, base : base + TILE] = -(factor * lc)
        lf[ROWS:, :] = jnp.zeros((PADDED - ROWS, 3 * TILE), F32)
        grad = lax.dot_general(lf[...].astype(BF16), vh[...], (((0,), (0,)), ((), ())), preferred_element_type=F32)
        u = uf[h]
        gx_ = jnp.sum(u * grad[TILE : 2 * TILE], axis=0, keepdims=True)
        gy_ = jnp.sum(u * grad[2 * TILE :], axis=0, keepdims=True)
        curl = (u[:64] * grad[64:TILE] - u[64:] * grad[:64]) * nz
        return elong, gx_, gy_, jnp.sum(curl, axis=0, keepdims=True)

    mine_half = field(core)
    landed(full.at[other], gc_r)
    elong, long_x, long_y, long_z = (p + q for p, q in zip(mine_half, field(other)))
    out_ref[0] = fpair[0:1, :] - (two_pi / (cols_x * WIDTH)) * long_x
    out_ref[1] = fpair[1:2, :] - (two_pi / (cols_y * WIDTH)) * long_y
    out_ref[2] = fpair[2:3, :] - (two_pi / (NBLK * DEPTH)) * long_z

    landed(e_p.at[1:], ep_r)
    esum = e_p[0]
    for s in range(1, XS * ys):
        esum = esum + e_p[s]
    etot = 0.5 * jnp.sum(elong, axis=0, keepdims=True) + esum
    etot = jnp.sum(etot, axis=1, keepdims=True) * (1.0 / (cols_x * cols_y * ATOMS))
    out_ref[3] = jnp.broadcast_to(etot, (1, ATOMS))
    left(hood.at[0:8], halo_s)
    left(mine.at[0], rc_s)
    left(recv_p.at[1:], rp_s)
    left(recv_z.at[1:], rz_s)
    left(gath_p.at[1:], gp_s)
    left(full.at[core], gc_s)
    left(e_z.at[1:], ez_s)
    left(e_p.at[1:], ep_s)


def column(sizes, positions, features, nbr_tiles, kvec_index, weight_charge, weight_pair):
    cols_x, cols_y, ys, z_lo_n, z_hi_n = sizes
    zs = z_lo_n * z_hi_n
    ps = XS * ys
    sub = PART // ys
    vmem, dma = pltpu.VMEM, pltpu.SemaphoreType.DMA
    scratch = [
        vmem((3, 1, ATOMS), F32),
        vmem((128, ATOMS), BF16),
        vmem((NBLK, 1, 32), jnp.int32),
        vmem((3, KVEC), jnp.int32),
        vmem((QCH, 128), BF16),
        vmem((PCH, 128), BF16),
        vmem((9, PCH + 3, ATOMS), F32),
        vmem((CORES, XS, PART, TILE), F32),
        vmem((XS, PART, TILE), F32),
        vmem((PART, TILE), F32),
        vmem((XS, ys, sub, TILE), F32),
        vmem((ps, sub, TILE), F32),
        vmem((zs, sub, TILE), F32),
        vmem((ps, sub, TILE), F32),
        vmem((CORES, XS, PART, TILE), F32),
        vmem((CORES * zs, 1, TILE), F32),
        vmem((ps, 1, TILE), F32),
        vmem((PADDED, ATOMS), F32),
        vmem((PADDED, ATOMS), BF16),
        vmem((CORES, TILE, ATOMS), F32),
        vmem((2 * TILE, ATOMS), BF16),
        vmem((PADDED, 3 * TILE), F32),
        vmem((2, PAIRS, TILE), F32),
        vmem((8, KVEC), jnp.int32),
        vmem((ATOMS, 3 * PCH), BF16),
        vmem((3, ATOMS, TILE), F32),
        vmem((32, ATOMS), F32),
        vmem((2, ATOMS, ATOMS), F32),
        vmem((3, ATOMS, TILE), F32),
        vmem((32, TILE), F32),
        vmem((8, ATOMS), F32),
        dma((6,)),
    ]
    one, each_x = dma(()), dma((XS,))
    scratch += [one, one, one, one, one, each_x, one, one, one, one, one, each_x, one, one, one, one, one, one]
    anywhere = pl.BlockSpec(memory_space=pl.ANY)
    out = pl.pallas_call(
        functools.partial(kernel, sizes),
        out_shape=pltpu.VMEM((4, 1, ATOMS), F32),
        in_specs=[anywhere] * 6,
        out_specs=pl.BlockSpec(memory_space=pltpu.VMEM),
        scratch_shapes=scratch,
        compiler_params=pltpu.CompilerParams(
            collective_id=0, has_side_effects=True, vmem_limit_bytes=60 * 1024 * 1024
        ),
    )(
        positions.reshape(3, 1, ATOMS),
        features[0, 0],
        nbr_tiles.reshape(NBLK, 1, 32),
        kvec_index,
        weight_charge,
        weight_pair,
    )
    return out[3, 0, 0], out[:3].reshape(1, 1, 3, ATOMS)


def solution(mesh):
    cols_x, cols_y = mesh.shape["gx"], mesh.shape["gy"]
    z_lo_n = 2
    sizes = (cols_x, cols_y, cols_x // z_lo_n, z_lo_n, cols_y // (XS * CORES))
    cell = P("gx", "gy", None, None)
    return jax.shard_map(
        functools.partial(column, sizes),
        mesh=mesh,
        in_specs=(cell, cell, cell, P(), P(), P()),
        out_specs=(P(), cell),
        check_vma=False,
    )
```

```python
import functools
import math

import jax
import jax.numpy as jnp
from jax import lax
from jax.experimental import pallas as pl
from jax.experimental.pallas import tpu as pltpu
from jax.sharding import PartitionSpec as P

WIDTH = 10.0
DEPTH = 12.0
CUT = 5.0
SMEAR = 1.5
SCALE = 0.25
NMAX = 8
TILE = 128
NBLK = 3
ATOMS = NBLK * TILE
QCH = 16
PCH = 16
KVEC = 4096
XS = 4
CORES = 2
TILES_C = 19
TILES_S = 18
ROWS = 8 * (TILES_C + TILES_S)
PAIRS = 8 * TILES_C
PADDED = 320
PART = PADDED // XS
MESH = pl.DeviceIdType.MESH
F32 = jnp.float32
BF16 = jnp.bfloat16
FAR = -1.0e30


def split(value):
    high = value.astype(BF16)
    return high, (value - high.astype(F32)).astype(BF16)


def unit_circle(turns):
    turns = turns - jnp.round(turns)
    half = turns * math.pi
    sq = half * half
    sine = 1.0 / 6227020800.0
    for term in (-1.0 / 39916800.0, 1.0 / 362880.0, -1.0 / 5040.0, 1.0 / 120.0, -1.0 / 6.0, 1.0):
        sine = sine * sq + term
    sine = sine * half
    cosine = 1.0 / 479001600.0
    for term in (-1.0 / 3628800.0, 1.0 / 40320.0, -1.0 / 720.0, 1.0 / 24.0, -0.5, 1.0):
        cosine = cosine * sq + term
    return 1.0 - 2.0 * sine * sine, 2.0 * sine * cosine


def kernel(
    sizes,
    pos_hbm,
    feat_hbm,
    nbr_hbm,
    kidx_hbm,
    wc_hbm,
    wp_hbm,
    out_ref,
    pos_ref,
    feat_ref,
    nbr_ref,
    kidx_ref,
    wc_ref,
    wp_ref,
    hood,
    mine,
    recv_c,
    acc_x,
    send_p,
    recv_p,
    recv_z,
    gath_p,
    full,
    e_z,
    e_p,
    vf,
    vh,
    uf,
    uh,
    lf,
    coef,
    codes,
    fi,
    pi,
    cmask,
    mbuf,
    acc_p,
    acc_e,
    fpair,
    in_s,
    halo_s,
    halo_x,
    halo_y,
    halo_d,
    rc_s,
    rc_r,
    rp_s,
    rp_r,
    rz_s,
    rz_r,
    gp_s,
    gp_r,
    gc_s,
    gc_r,
    ez_s,
    ez_r,
    ep_s,
    ep_r,
):
    cols_x, cols_y, ys, z_lo_n, z_hi_n = sizes
    zs = z_lo_n * z_hi_n
    sub = PART // ys
    gx = lax.axis_index("gx")
    gy = lax.axis_index("gy")
    z_lo, y = lax.div(gx, ys), lax.rem(gx, ys)
    z_hi = lax.div(gy, XS * CORES)
    x = lax.div(lax.rem(gy, XS * CORES), CORES)
    core = lax.rem(gy, CORES)
    z = z_hi * z_lo_n + z_lo
    other = 1 - core
    me = x * ys + y

    inputs = []
    pairs = ((feat_hbm, feat_ref), (wp_hbm, wp_ref), (pos_hbm, pos_ref), (wc_hbm, wc_ref), (nbr_hbm, nbr_ref), (kidx_hbm, kidx_ref))
    for i, (src, dst) in enumerate(pairs):
        cp = pltpu.make_async_copy(src, dst, in_s.at[i])
        cp.start()
        inputs.append(cp)

    core_dev = (gx, gy + 1 - 2 * core)

    def plane_dev(j, k):
        return (z_lo * ys + k, (z_hi * XS + j) * CORES + core)

    def z_dev(j, core=core):
        lo, hi = lax.rem(j, z_lo_n), lax.div(j, z_lo_n)
        return (lo * ys + y, (hi * XS + x) * CORES + core)

    def halo_dev(ix, iy):
        return (
            lax.rem(gx + (1 - ix) + cols_x, cols_x),
            lax.rem(gy + (1 - iy) + cols_y, cols_y),
        )

    def around(value, step, size):
        return lax.rem(value + step, size) if step else value

    halo = [(0, 1), (2, 1), (1, 0), (1, 2)]
    x_order = [around(x, d, XS) for d in range(XS)]
    y_order = [around(y, d, ys) for d in range(ys)]
    plane = [(j, k) for n, j in enumerate(x_order) for m, k in enumerate(y_order) if n or m]
    hops = lambda jk: min(jk[0], XS - jk[0]) + min(jk[1], ys - jk[1])
    outward = sorted([(j, k) for j in range(XS) for k in range(ys)], key=hops)
    z_peers = [around(z, d, zs) for d in range(1, zs)]

    def copy(src, dst, send, recv, dev):
        return pltpu.make_async_remote_copy(
            src_ref=src, dst_ref=dst, send_sem=send, recv_sem=recv, device_id=dev, device_id_type=MESH
        )

    barrier = pltpu.get_barrier_semaphore()
    steps = [(n, m) for n in range(XS) for m in range(ys) if n or m]
    steps = sorted(steps, key=lambda nm: -(min(nm[0], XS - nm[0]) + min(nm[1], ys - nm[1])))
    partners = [plane_dev(x_order[n], y_order[m]) for n, m in steps]
    partners += [z_dev(z_peers[d - 1]) for d in sorted(range(1, zs), key=lambda d: -min(d, zs - d))]
    partners += [z_dev(j, other) for j in z_peers]
    partners += [core_dev]
    partners += [halo_dev(ix, iy) for ix, iy in halo]
    for dev in partners:
        pl.semaphore_signal(barrier, inc=1, device_id=dev, device_id_type=MESH)

    def landed(ref, sem):
        copy(ref, ref, sem, sem, core_dev).wait_recv()

    def left(ref, sem):
        copy(ref, ref, sem, sem, core_dev).wait_send()


    for cp in inputs[:3]:
        cp.wait()
    feat = feat_ref[...]
    pair_feat = jnp.dot(wp_ref[...], feat, preferred_element_type=F32)
    hood[4, 0:PCH, :] = pair_feat
    for i in range(3):
        hood[4, PCH + i : PCH + i + 1, :] = pos_ref[i] * (1.0 / CUT)
    inputs[3].wait()
    charges = jnp.dot(wc_ref[...], feat, preferred_element_type=F32).astype(BF16).astype(F32)
    order = lax.broadcasted_iota(jnp.int32, (8, ATOMS), 0).astype(F32) + 1.0
    gxf, gyf = gx.astype(F32), gy.astype(F32)
    cx, sx = unit_circle(order * ((pos_ref[0] + gxf * WIDTH) * (1.0 / (cols_x * WIDTH))))
    cy, sy = unit_circle(order * ((pos_ref[1] + gyf * WIDTH) * (1.0 / (cols_y * WIDTH))))
    cz, sz = unit_circle(order * (pos_ref[2] * (1.0 / (NBLK * DEPTH))))

    def row(tile):
        return pl.ds(8 * tile, 8)

    for n in range(1, NMAX + 1):
        cyn, syn = cy[n - 1 : n], sy[n - 1 : n]
        cc, ss, sc, cs = cx * cyn, sx * syn, sx * cyn, cx * syn
        vf[row(8 + n), :] = cc - ss
        vf[row(8 - n), :] = cc + ss
        vf[row(TILES_C + 8 + n), :] = sc + cs
        vf[row(TILES_C + 8 - n), :] = sc - cs
    vf[row(8), :] = cx
    vf[row(TILES_C + 8), :] = sx
    vf[row(17), :] = cy
    vf[row(TILES_C + 17), :] = sy
    vf[row(18), :] = jnp.where(order < 1.5, 1.0, 0.0)
    vf[ROWS:, :] = jnp.zeros((PADDED - ROWS, ATOMS), F32)
    for c in range(QCH):
        h, first = c // 8, 8 * (c % 8)
        uf[h, first : first + 8, :] = cz * charges[c : c + 1]
        uf[h, 64 + first : 72 + first, :] = sz * charges[c : c + 1]
    vh[...] = vf[...].astype(BF16)
    uh[...] = uf[...].reshape(2 * TILE, ATOMS).astype(BF16)

    rotated = [x_order[i] for i in (2, 1, 3, 0)]
    far = [y_order[i] for i in sorted(range(ys), key=lambda i: -min(i, ys - i))]
    for j in rotated:
        rows = pl.ds(pl.multiple_of(j * PART, PART), PART)
        part = lax.dot_general(vh[rows, :], uh[...], (((1,), (1,)), ((), ())), preferred_element_type=F32)
        mine[0, j] = part[:, :TILE]
        mine[1, j] = part[:, TILE:]

    pl.semaphore_wait(barrier, len(partners))
    for ix, iy in halo:
        k = 3 * ix + iy
        copy(hood.at[4], hood.at[k], halo_s, halo_x if iy == 1 else halo_y, halo_dev(ix, iy)).start()


    for j in rotated:
        copy(mine.at[other, j], recv_c.at[j], rc_s, rc_r.at[j], core_dev).start()
    for j in rotated:
        landed(recv_c.at[j], rc_r.at[j])
        acc_x[...] = mine[core, j] + recv_c[j]
        for k in range(ys):
            send_p[j, k] = acc_x[sub * k : sub * (k + 1), :]
        for k in far:
            if j is x and k is y:
                recv_p[me] = send_p[x, y]
            else:
                copy(send_p.at[j, k], recv_p.at[me], rp_s, rp_r, plane_dev(j, k)).start()

    fhigh, flow = split(pair_feat)
    stacked = jnp.concatenate([fhigh, flow, fhigh], axis=0).astype(F32)
    fi[...] = jnp.transpose(stacked).astype(BF16)
    own_pos = [pos_ref[i] * (1.0 / CUT) for i in range(3)] + [jnp.zeros((5, ATOMS), F32)]
    own_pos = jnp.transpose(jnp.concatenate(own_pos, axis=0))
    for i in range(3):
        pi[i] = jnp.broadcast_to(own_pos[:, i : i + 1], (ATOMS, TILE))
    inputs[4].wait()
    tile_id = lax.broadcasted_iota(jnp.int32, (32, 32), 0)
    for b in range(NBLK):
        found = jnp.where(nbr_ref[b] == tile_id, 1.0, FAR)
        found = jnp.max(found, axis=1, keepdims=True)
        cmask[:, b * TILE : (b + 1) * TILE] = jnp.broadcast_to(found, (32, TILE))
    acc_p[...] = jnp.zeros((3, ATOMS, TILE), F32)
    acc_e[...] = jnp.zeros((32, TILE), F32)
    wrap = NBLK * DEPTH / CUT

    def couple(k, slot):
        high, low = split(hood[k, 0:PCH, :])
        fj = jnp.concatenate([high, high, low], axis=0)
        mbuf[slot] = jnp.dot(fi[...], fj, preferred_element_type=F32)

    def pair_column(k, slot, energy=True, force=True):
        shift_x = (lax.div(k, 3) - 1).astype(F32) * (WIDTH / CUT)
        shift_y = (lax.rem(k, 3) - 1).astype(F32) * (WIDTH / CUT)
        xj = hood[k, PCH : PCH + 1, :] + shift_x
        yj = hood[k, PCH + 1 : PCH + 2, :] + shift_y
        zj = hood[k, PCH + 2 : PCH + 3, :]
        limits = [cmask[pl.ds(NBLK * k + c, 1), :] for c in range(NBLK)]
        ae = acc_e[...]
        for b in range(NBLK):
            for g in range(TILE // 32):
                rows = slice(b * TILE + 32 * g, b * TILE + 32 * g + 32)
                xi, yi, zi = pi[0, rows, :], pi[1, rows, :], pi[2, rows, :]
                if force:
                    ax, ay, az = acc_p[0, rows, :], acc_p[1, rows, :], acc_p[2, rows, :]
                for c in range(NBLK):
                    cols = slice(c * TILE, (c + 1) * TILE)
                    zc = zj[:, cols]
                    if c - b == 2:
                        zc = zc - wrap
                    if b - c == 2:
                        zc = zc + wrap
                    limit = limits[c][:, b * TILE : (b + 1) * TILE]
                    dx, dy, dz = xi - xj[:, cols], yi - yj[:, cols], zi - zc
                    w = jnp.maximum(limit - (dx * dx + dy * dy + dz * dz), 0.0)
                    mw = mbuf[slot, rows, cols] * w
                    if force:
                        ax = ax + mw * dx
                        ay = ay + mw * dy
                        az = az + mw * dz
                    if energy:
                        ae = ae + mw * w
                if force:
                    acc_p[0, rows, :] = ax
                    acc_p[1, rows, :] = ay
                    acc_p[2, rows, :] = az
        if energy:
            acc_e[...] = ae

    landed(hood.at[0:2], halo_x)
    for ix in (0, 2):
        for iy in (0, 2):
            copy(hood.at[3 * ix + 1], hood.at[3 * ix + iy], halo_s, halo_d, halo_dev(1, iy)).start()
    couple(4, 0)
    pair_column(jnp.int32(4), 0)
    landed(hood.at[0:2], halo_y)

    def pair_columns(column_of, **parts):
        couple(column_of(0), 0)

        def pair_step(i, carry):
            slot = lax.rem(i, 2)
            couple(column_of(i + 1), 1 - slot)
            pair_column(column_of(i), slot, **parts)
            return carry

        lax.fori_loop(0, 3, pair_step, 0)
        pair_column(jnp.int32(column_of(3)), 1, **parts)

    pair_columns(lambda i: 2 * i + 1)

    landed(recv_p.at[1:], rp_r)
    total = recv_p[0]
    for s in range(1, XS * ys):
        total = total + recv_p[s]

    recv_z[z] = total
    for j in sorted(range(zs), key=lambda j: min(j, zs - j)):

        @pl.when(j != z)
        def _(j=j):
            copy(recv_z.at[z], recv_z.at[z], rz_s, rz_r, z_dev(j)).start()


    landed(hood.at[0:4], halo_d)

    def corner(i):
        return 2 * i + 2 * (i // 2 if isinstance(i, int) else lax.div(i, 2))

    pair_columns(corner, force=False)
    own = jnp.sum(pair_feat * pair_feat, axis=0, keepdims=True)
    epart = jnp.sum(acc_e[...], axis=0, keepdims=True)
    for b in range(NBLK):
        blk = slice(b * TILE, (b + 1) * TILE)
        named = jnp.maximum(cmask[4 * NBLK + b : 4 * NBLK + b + 1, blk], 0.0)
        epart = epart - named * own[:, blk]
    part = z * CORES + core
    e_z[part] = epart * (0.5 * SCALE)
    for j in z_peers:
        copy(e_z.at[part], e_z.at[part], ez_s, ez_r, z_dev(j)).start()
        copy(e_z.at[part], e_z.at[part], ez_s, ez_r, z_dev(j, other)).start()
    copy(e_z.at[part], e_z.at[part], ez_s, ez_r, core_dev).start()
    landed(recv_z.at[1:], rz_r)
    total = recv_z[0]
    for j in range(1, zs):
        total = total + recv_z[j]

    gath_p[me] = total
    for j, k in outward:

        @pl.when(j * ys + k != me)
        def _(j=j, k=k):
            copy(gath_p.at[me], gath_p.at[me], gp_s, gp_r.at[x], plane_dev(j, k)).start()

    inputs[5].wait()
    kx, ky, kz = kidx_ref[0:1, :], kidx_ref[1:2, :], kidx_ref[2:3, :]
    codes[0:1, :] = kx * 17 + ky
    codes[1:2, :] = kz
    coef[...] = jnp.zeros((2, PAIRS, TILE), F32)
    step = 512
    row_id = lax.broadcasted_iota(jnp.int32, (PAIRS, 1), 0)
    tile_of, sub_of = lax.div(row_id, 8), lax.rem(row_id, 8)
    nx = jnp.where(tile_of < 17, sub_of + 1, 0)
    ny = jnp.where(tile_of < 17, tile_of - 8, jnp.where(tile_of == 17, sub_of + 1, 0))
    none = 100000
    code = nx * 17 + ny
    plus = jnp.where((tile_of == 18) & (sub_of > 0), none, code)
    minus = jnp.where(tile_of == 18, none, -code)
    nz_of = lax.rem(lax.broadcasted_iota(jnp.int32, (TILE, 1), 0), 8) + 1

    def count(i, carry):
        cols = pl.ds(pl.multiple_of(i * step, step), step)
        xy, zc = codes[0:1, cols], codes[1:2, cols]
        on_z = jnp.where(zc == nz_of, 1.0, 0.0).astype(BF16)
        for s, target in ((0, plus), (1, minus)):
            on_xy = jnp.where(xy == target, 1.0, 0.0).astype(BF16)
            coef[s] += lax.dot_general(on_xy, on_z, (((1,), (1,)), ((), ())), preferred_element_type=F32)
        return carry

    lax.fori_loop(0, KVEC // step, count, 0)
    two_pi = 2.0 * math.pi
    wx = nx.astype(F32) * (two_pi / (cols_x * WIDTH))
    wy = ny.astype(F32) * (two_pi / (cols_y * WIDTH))
    wz = (lax.rem(lax.broadcasted_iota(jnp.int32, (1, TILE), 1), 8) + 1).astype(F32) * (two_pi / (NBLK * DEPTH))
    ksq = (wx * wx + wy * wy) + wz * wz
    norm = 1.0 / math.sqrt(cols_x * cols_y * ATOMS * KVEC)
    green = 4.0 * norm * jnp.exp(-0.5 * SMEAR * SMEAR * ksq) / ksq
    cplus, cminus = coef[0], coef[1]
    coef[0] = green * (cplus + cminus)
    lanes = lax.broadcasted_iota(jnp.int32, (1, TILE), 1)
    coef[1] = jnp.where(lanes < 64, -green, green) * (cplus - cminus)

    landed(e_z.at[1:], ez_r)
    esum = e_z[0]
    for j in range(1, CORES * zs):
        esum = esum + e_z[j]
    e_p[me] = esum
    for j, k in plane:
        copy(e_p.at[me], e_p.at[me], ep_s, ep_r, plane_dev(j, k)).start()
    pair_columns(corner, energy=False)
    force_scale = 4.0 * SCALE / CUT
    ones = jnp.ones((8, TILE), BF16)
    for i in range(3):
        high, low = split(acc_p[i])
        sums = lax.dot_general(ones, high, (((1,), (1,)), ((), ())), preferred_element_type=F32)
        sums = sums + lax.dot_general(ones, low, (((1,), (1,)), ((), ())), preferred_element_type=F32)
        fpair[i : i + 1, :] = force_scale * sums[0:1]

    for j in [x_order[i] for i in (0, 1, 3, 2)]:
        landed(gath_p.at[pl.ds(j * ys, ys - 1 if j is x else ys)], gp_r.at[j])
        for k in range(ys):
            full[core, j, sub * k : sub * (k + 1), :] = gath_p[j * ys + k]
        copy(full.at[core, j], full.at[core, j], gc_s, gc_r, core_dev).start()
    sub_id = lax.broadcasted_iota(jnp.int32, (8, TILE), 0).astype(F32) + 1.0
    nz = (lax.rem(lax.broadcasted_iota(jnp.int32, (64, 1), 0), 8) + 1).astype(F32)

    def field(h):
        def tile_of(t):
            return full[h, (8 * t) // PART, (8 * t) % PART : (8 * t) % PART + 8, :]

        elong = jnp.zeros((8, TILE), F32)
        for t in range(TILES_C):
            a, b = coef[0, 8 * t : 8 * t + 8, :], coef[1, 8 * t : 8 * t + 8, :]
            rc, rs = row(t), row(TILES_C + t)
            xc = tile_of(t)
            if t == TILES_S:
                lc = a * xc
                elong = elong + lc * xc
                lf[rc, 0:TILE] = lc
                lf[rc, TILE:] = jnp.zeros((8, 2 * TILE), F32)
                continue
            xs = tile_of(TILES_C + t)
            lc = a * xc + b * pltpu.roll(xs, 64, 1)
            ls = a * xs - b * pltpu.roll(xc, 64, 1)
            elong = elong + (lc * xc + ls * xs)
            lf[rc, 0:TILE] = lc
            lf[rs, 0:TILE] = ls
            fx = sub_id if t < 17 else 0.0
            fy = float(t - 8) if t < 17 else sub_id
            for base, factor in ((TILE, fx), (2 * TILE, fy)):
                lf[rc, base : base + TILE] = factor * ls
                lf[rs, base : base + TILE] = -(factor * lc)
        lf[ROWS:, :] = jnp.zeros((PADDED - ROWS, 3 * TILE), F32)
        grad = lax.dot_general(lf[...].astype(BF16), vh[...], (((0,), (0,)), ((), ())), preferred_element_type=F32)
        u = uf[h]
        gx_ = jnp.sum(u * grad[TILE : 2 * TILE], axis=0, keepdims=True)
        gy_ = jnp.sum(u * grad[2 * TILE :], axis=0, keepdims=True)
        curl = (u[:64] * grad[64:TILE] - u[64:] * grad[:64]) * nz
        return elong, gx_, gy_, jnp.sum(curl, axis=0, keepdims=True)

    mine_half = field(core)
    landed(full.at[other], gc_r)
    elong, long_x, long_y, long_z = (p + q for p, q in zip(mine_half, field(other)))
    out_ref[0] = fpair[0:1, :] - (two_pi / (cols_x * WIDTH)) * long_x
    out_ref[1] = fpair[1:2, :] - (two_pi / (cols_y * WIDTH)) * long_y
    out_ref[2] = fpair[2:3, :] - (two_pi / (NBLK * DEPTH)) * long_z

    landed(e_p.at[1:], ep_r)
    esum = e_p[0]
    for s in range(1, XS * ys):
        esum = esum + e_p[s]
    etot = 0.5 * jnp.sum(elong, axis=0, keepdims=True) + esum
    etot = jnp.sum(etot, axis=1, keepdims=True) * (1.0 / (cols_x * cols_y * ATOMS))
    out_ref[3] = jnp.broadcast_to(etot, (1, ATOMS))
    left(hood.at[0:8], halo_s)
    left(mine.at[0], rc_s)
    left(recv_p.at[1:], rp_s)
    left(recv_z.at[1:], rz_s)
    left(gath_p.at[1:], gp_s)
    left(full.at[core], gc_s)
    left(e_z.at[1:], ez_s)
    left(e_p.at[1:], ep_s)


def column(sizes, positions, features, nbr_tiles, kvec_index, weight_charge, weight_pair):
    cols_x, cols_y, ys, z_lo_n, z_hi_n = sizes
    zs = z_lo_n * z_hi_n
    ps = XS * ys
    sub = PART // ys
    vmem, dma = pltpu.VMEM, pltpu.SemaphoreType.DMA
    scratch = [
        vmem((3, 1, ATOMS), F32),
        vmem((128, ATOMS), BF16),
        vmem((NBLK, 1, 32), jnp.int32),
        vmem((3, KVEC), jnp.int32),
        vmem((QCH, 128), BF16),
        vmem((PCH, 128), BF16),
        vmem((9, PCH + 3, ATOMS), F32),
        vmem((CORES, XS, PART, TILE), F32),
        vmem((XS, PART, TILE), F32),
        vmem((PART, TILE), F32),
        vmem((XS, ys, sub, TILE), F32),
        vmem((ps, sub, TILE), F32),
        vmem((zs, sub, TILE), F32),
        vmem((ps, sub, TILE), F32),
        vmem((CORES, XS, PART, TILE), F32),
        vmem((CORES * zs, 1, TILE), F32),
        vmem((ps, 1, TILE), F32),
        vmem((PADDED, ATOMS), F32),
        vmem((PADDED, ATOMS), BF16),
        vmem((CORES, TILE, ATOMS), F32),
        vmem((2 * TILE, ATOMS), BF16),
        vmem((PADDED, 3 * TILE), F32),
        vmem((2, PAIRS, TILE), F32),
        vmem((8, KVEC), jnp.int32),
        vmem((ATOMS, 3 * PCH), BF16),
        vmem((3, ATOMS, TILE), F32),
        vmem((32, ATOMS), F32),
        vmem((2, ATOMS, ATOMS), F32),
        vmem((3, ATOMS, TILE), F32),
        vmem((32, TILE), F32),
        vmem((8, ATOMS), F32),
        dma((6,)),
    ]
    one, each_x = dma(()), dma((XS,))
    scratch += [one, one, one, one, one, each_x, one, one, one, one, one, each_x, one, one, one, one, one, one]
    anywhere = pl.BlockSpec(memory_space=pl.ANY)
    out = pl.pallas_call(
        functools.partial(kernel, sizes),
        out_shape=pltpu.VMEM((4, 1, ATOMS), F32),
        in_specs=[anywhere] * 6,
        out_specs=pl.BlockSpec(memory_space=pltpu.VMEM),
        scratch_shapes=scratch,
        compiler_params=pltpu.CompilerParams(
            collective_id=0, has_side_effects=True, vmem_limit_bytes=60 * 1024 * 1024
        ),
    )(
        positions.reshape(3, 1, ATOMS),
        features[0, 0],
        nbr_tiles.reshape(NBLK, 1, 32),
        kvec_index,
        weight_charge,
        weight_pair,
    )
    return out[3, 0, 0], out[:3].reshape(1, 1, 3, ATOMS)


def solution(mesh):
    cols_x, cols_y = mesh.shape["gx"], mesh.shape["gy"]
    z_lo_n = 2
    sizes = (cols_x, cols_y, cols_x // z_lo_n, z_lo_n, cols_y // (XS * CORES))
    cell = P("gx", "gy", None, None)
    return jax.shard_map(
        functools.partial(column, sizes),
        mesh=mesh,
        in_specs=(cell, cell, cell, P(), P(), P()),
        out_specs=(P(), cell),
        check_vma=False,
    )
```
